32 devices in a mesh: node: 8 (over y, x, core), local: 4 (over z).
Axes of the slice: x: 2, y: 2, z: 4, core: 2. Of those that a mesh axis runs over, the one named last changes fastest.
Arguments:
- tokens: bfloat16 [256, 7168], P(('node', 'local')), may hold values from -6 to 6
- grad_out: bfloat16 [256, 7168], P(('node', 'local')), may hold values from -6 to 6
- expert_ids: int32 [256, 4], P(('node', 'local')), may hold values from 0 to 7, all different within a row; in each aligned block of 8 rows (0 to 7, 8 to 15, ...) at most 8 rows name the same one
- gate_weights: bfloat16 [256, 4], P(('node', 'local')), may hold values from 0.049804688 to 1
- w_gate: bfloat16 [8, 7168, 1024], P('node', None, 'local'), may hold values from -0.0625 to 0.0625
- w_up: bfloat16 [8, 7168, 1024], P('node', None, 'local'), may hold values from -0.0625 to 0.0625
- w_down: bfloat16 [8, 1024, 7168], P('node', 'local'), may hold values from -0.1875 to 0.1875
Outputs:
- grad_in: bfloat16 [256, 7168], P(('node', 'local'))
- grad_gate: bfloat16 [256, 4], P(('node', 'local'))
- grad_w_gate: bfloat16 [8, 7168, 1024], P('node', None, 'local')
- grad_w_up: bfloat16 [8, 7168, 1024], P('node', None, 'local')
- grad_w_down: bfloat16 [8, 1024, 7168], P('node', 'local')
The draws below stay inside these ranges and needn't reach their ends.
Inputs may be any that keep to these rules, and one draw needn't show every extreme that they name: `expert_ids`: the 4 experts of a token differ. Among one device's 8 tokens no expert is named more than 8 times, and in every draw some expert is named exactly 8 times by some device.
All inputs are finite; a program needn't handle non-finite values.
Results may differ from the reference program's by a relative error of at most 0.024.
Values may be sent and summed in bfloat16 or wider, within the bound.
No kernel may reach another device: no remote copies, remote signals or barrier semaphores. Data moves between devices by JAX's collectives and lax.ppermute only.
A program may use at most 128 MiB of HBM per device.

```python
import math
import jax
import jax.numpy as jnp
import numpy as np
from jax import lax

D = 7168
HID = 1024
TOP = 4
TOK_DEV = 8
EXPERTS = 8
HID_DEV = 256
CAP = 8
TOKENS = 256
N_LOCAL = 4
DEVICES = 32


def level_of(rng, dims, shards, smallest, high):
    gain, own = 1.0, jax.random.fold_in(rng, 6)
    for position, parts in shards:
        draws = jnp.exp(jax.random.uniform(jax.random.fold_in(own, position), (parts,), jnp.float32, smallest / len(shards), high / len(shards)))
        gain = gain * jnp.repeat(draws, dims[position] // parts).reshape([-1 if axis == position else 1 for axis in range(len(dims))])
    return gain


def shared_out(stream_key, own, number, rows, number_of, top, reach, lean):
    order = jax.random.permutation(stream_key, number_of)
    crowded, common = portions_of(number_of, rows * top, reach, lean, True), portions_of(number_of, rows * top, reach, lean, False)
    places = jnp.arange(number_of)

    def named(sizes, rotation):
        used = int((sizes > 0).sum())
        fixed = max(1, used // 4)
        moved = fixed + (places - fixed + rotation * (used - fixed)) % max(1, number_of - fixed)
        return jnp.zeros((number_of,), jnp.int32).at[order[jnp.where(places < fixed, places, moved)]].set(jnp.asarray(sizes, jnp.int32))

    sizes = jnp.where(number % 4 == 0, named(crowded, number // 4), named(common, number - number // 4 - 1))
    mixed = jax.random.permutation(jax.random.fold_in(own, 3), number_of)
    giver, receiver = mixed[0:number_of // 2 * 2:2], mixed[1:number_of // 2 * 2:2]
    slack = jnp.minimum(sizes[giver] - 1, reach - sizes[receiver]) // 2
    slack = jnp.where((giver == order[0]) | (receiver == order[0]) | (sizes[receiver] == 0), 0, jnp.maximum(slack, 0))
    moved = jax.random.randint(jax.random.fold_in(own, 4), (number_of // 2,), 0, 1 << 20) % (slack + 1)
    sizes = sizes.at[giver].add(-moved).at[receiver].add(moved)
    labels = jnp.searchsorted(jnp.cumsum(sizes), jnp.arange(rows * top), side="right").astype(jnp.int32)
    listing = labels.reshape(top, rows).T
    listing = listing[jax.random.permutation(jax.random.fold_in(own, 1), rows)]
    rotation = jax.random.randint(jax.random.fold_in(own, 2), (rows, 1), 0, top)
    return jnp.take_along_axis(listing, (jnp.arange(top)[None, :] + rotation) % top, axis=1)


def portions_of(amount, total, limit, lean, full):
    weights = [(1 << 20) // math.isqrt(grade ** lean) + 1 for grade in range(1, amount + 1)]
    largest = limit if full else min(limit, max(-(-total // amount), total * weights[0] // sum(weights)))
    least = 1 if total - largest >= amount - 1 else 0
    counts, spare = [largest] + [least] * (amount - 1), total - largest - least * (amount - 1)
    while spare > 0:
        free = [i for i in range(1, amount) if counts[i] < largest] or [i for i in range(1, amount) if counts[i] < limit]
        whole, left = sum([weights[i] for i in free]), spare
        for i in free:
            more = min(limit - counts[i], max(1, left * weights[i] // whole), spare)
            counts[i] = counts[i] + more
            spare = spare - more
    return np.array(counts)


def noise(own_key, dims, deviation, reach, shards=(), kind=jnp.bfloat16):
    level = level_of(own_key, dims, shards, -0.22, 0.18) if shards else 1.0
    values = jax.random.normal(own_key, dims, jnp.float32) * deviation * level
    return jnp.minimum(jnp.maximum(values, -reach), reach).astype(kind)


def setup_inputs(seed: int = 0) -> dict:
    streams_of = jax.random.split(jax.random.key(seed), 8)
    tokens = noise(streams_of[0], (TOKENS, D), 1.0, 6.0, ((0, 32),))
    grad_out = noise(streams_of[1], (TOKENS, D), 1.0, 6.0, ((0, 32),))
    expert_ids_keys = jax.random.split(jax.random.fold_in(streams_of[2], 1), TOKENS // TOK_DEV)
    expert_ids_turns = jax.random.permutation(jax.random.fold_in(streams_of[2], 3), TOKENS // TOK_DEV)
    expert_ids = jax.vmap(lambda own, number: shared_out(jax.random.fold_in(streams_of[2], 2), own, number, TOK_DEV, EXPERTS, TOP, CAP, 2))(expert_ids_keys, expert_ids_turns).reshape((TOKENS, TOP))
    gate_weights = jnp.clip(jnp.exp(math.log(1.0) - 2.9996462 * jax.random.uniform(streams_of[3], (TOKENS, TOP), jnp.float32) ** level_of(streams_of[3], (TOKENS, TOP), ((0, 32),), -0.2, 0.2)), 0.049804688, 1.0).astype(jnp.bfloat16)
    w_gate = noise(streams_of[4], (EXPERTS, D, HID), D ** -0.5, 0.0625, ((0, 8), (2, 4)))
    w_up = noise(streams_of[5], (EXPERTS, D, HID), D ** -0.5, 0.0625, ((0, 8), (2, 4)))
    w_down = noise(streams_of[6], (EXPERTS, HID, D), HID ** -0.5, 0.1875, ((0, 8), (1, 4)))
    return {"tokens": tokens, "grad_out": grad_out, "expert_ids": expert_ids, "gate_weights": gate_weights, "w_gate": w_gate, "w_up": w_up, "w_down": w_down}


def silu_parts(gate_pre):
    sigmoid_val = jax.nn.sigmoid(gate_pre)
    return gate_pre * sigmoid_val, sigmoid_val * (1.0 + gate_pre * (1.0 - sigmoid_val))


def reference(tokens, grad_out, expert_ids, gate_weights, w_gate, w_up, w_down):
    onehot = (expert_ids[:, :, None] == jnp.arange(EXPERTS, dtype=jnp.int32)[None, None, :]).astype(jnp.int32)
    per_token = jnp.sum(onehot, axis=1).reshape(DEVICES, TOK_DEV, EXPERTS)
    earlier = (jnp.cumsum(per_token, axis=1) - per_token).reshape(TOKENS, EXPERTS)
    slot_index = jnp.sum(earlier[:, None, :] * onehot, axis=2).astype(jnp.int32)
    device_row = ((jnp.arange(TOKENS, dtype=jnp.int32) // TOK_DEV)[:, None] * CAP + slot_index).astype(jnp.int32)
    token_index = jnp.broadcast_to(jnp.arange(TOKENS, dtype=jnp.int32)[:, None], (TOKENS, TOP))
    choice_index = jnp.broadcast_to(jnp.arange(TOP, dtype=jnp.int32)[None, :], (TOKENS, TOP))
    rows_total = DEVICES * CAP
    table_token = jnp.zeros((EXPERTS, rows_total), jnp.int32).at[expert_ids, device_row].set(token_index)
    table_choice = jnp.zeros((EXPERTS, rows_total), jnp.int32).at[expert_ids, device_row].set(choice_index)
    table_live = jnp.zeros((EXPERTS, rows_total), jnp.int32).at[expert_ids, device_row].set(1)

    def compute_expert(expert):
        rows_token = table_token[expert]
        live = table_live[expert]
        rows_in = tokens[rows_token] * live[:, None].astype(tokens.dtype)
        rows_grad = grad_out[rows_token] * live[:, None].astype(grad_out.dtype)
        rows_gate = gate_weights[rows_token, table_choice[expert]].astype(jnp.float32) * live.astype(jnp.float32)
        gate_proj = w_gate[expert]
        up_proj = w_up[expert]
        down_proj = w_down[expert]
        gate_pre = jnp.dot(rows_in, gate_proj, preferred_element_type=jnp.float32)
        up_pre = jnp.dot(rows_in, up_proj, preferred_element_type=jnp.float32)
        activated, slope = silu_parts(gate_pre)
        hidden = (activated * up_pre).astype(jnp.bfloat16)
        grad_hidden = jnp.dot(rows_grad, down_proj.T, preferred_element_type=jnp.float32)
        shard_sums = jnp.sum((hidden.astype(jnp.float32) * grad_hidden).reshape(rows_total, N_LOCAL, HID_DEV), axis=2)
        shard_sums = lax.optimization_barrier(shard_sums.astype(jnp.bfloat16))
        gate_rows = jnp.sum(shard_sums.astype(jnp.float32), axis=1).astype(jnp.bfloat16)
        scaled = rows_gate[:, None] * grad_hidden
        grad_gate_pre = (scaled * up_pre * slope).astype(jnp.bfloat16)
        grad_up_pre = (scaled * activated).astype(jnp.bfloat16)
        weighted = (rows_gate[:, None] * hidden.astype(jnp.float32)).astype(jnp.bfloat16)
        grad_down = jnp.dot(weighted.T, rows_grad, preferred_element_type=jnp.float32).astype(jnp.bfloat16)
        grad_gate_w = jnp.dot(rows_in.T, grad_gate_pre, preferred_element_type=jnp.float32).astype(jnp.bfloat16)
        grad_up_w = jnp.dot(rows_in.T, grad_up_pre, preferred_element_type=jnp.float32).astype(jnp.bfloat16)
        partial_gate = jnp.einsum("rlh,dlh->lrd", grad_gate_pre.astype(jnp.float32).reshape(rows_total, N_LOCAL, HID_DEV), gate_proj.astype(jnp.float32).reshape(D, N_LOCAL, HID_DEV))
        partial_up = jnp.einsum("rlh,dlh->lrd", grad_up_pre.astype(jnp.float32).reshape(rows_total, N_LOCAL, HID_DEV), up_proj.astype(jnp.float32).reshape(D, N_LOCAL, HID_DEV))
        partial_value = lax.optimization_barrier((partial_gate + partial_up).astype(jnp.bfloat16))
        contrib = jnp.sum(partial_value.astype(jnp.float32), axis=0).astype(jnp.bfloat16)
        return contrib, gate_rows, grad_gate_w, grad_up_w, grad_down

    contrib, gate_rows, grad_w_gate, grad_w_up, grad_w_down = lax.map(compute_expert, jnp.arange(EXPERTS, dtype=jnp.int32))
    flat_token = table_token.reshape(-1)
    flat_choice = table_choice.reshape(-1)
    flat_live = table_live.reshape(-1).astype(jnp.float32)
    grad_in = jnp.zeros((TOKENS, D), jnp.float32).at[flat_token].add(contrib.reshape(-1, D).astype(jnp.float32) * flat_live[:, None]).astype(jnp.bfloat16)
    grad_gate = jnp.zeros((TOKENS, TOP), jnp.float32).at[flat_token, flat_choice].add(gate_rows.reshape(-1).astype(jnp.float32) * flat_live).astype(jnp.bfloat16)
    return grad_in, grad_gate, grad_w_gate, grad_w_up, grad_w_down
```

```python
import jax
import jax.numpy as jnp
from jax import lax
from jax.sharding import PartitionSpec as P

AXES = ("node", "local")
LANES = 128
CONTRACT_ROWS = (((0,), (0,)), ((), ()))
CONTRACT_COLS = (((1,), (1,)), ((), ()))
CHUNKS = 2


def permute(value, node_count, local_count, target):
    pairs = []
    for node in range(node_count):
        for place in range(local_count):
            to_node, to_place = target(node, place)
            pairs.append((node * local_count + place, to_node * local_count + to_place))
    return lax.ppermute(value, AXES, pairs)


def dense(tokens, grad_out, expert_ids, gate_weights, w_gate, w_up, w_down):
    tok_count, width = tokens.shape
    node_count = lax.axis_size("node")
    local_count = lax.axis_size("local")
    bits = [1 << i for i in range(1, node_count.bit_length() - 1)]
    steps = len(bits)

    def exchange(value, step):
        def target(node, place):
            bit = bits[step] if node % 2 == 0 else bits[steps - 1 - step]
            return node ^ bit, place

        return permute(value, node_count, local_count, target)

    def sibling(value):
        return permute(value, node_count, local_count, lambda n, p: (n ^ 1, p))

    def rotate(value, k):
        return permute(value, node_count, local_count, lambda n, p: (n, (p + k) % local_count))

    onehot = expert_ids[:, :, None] == jnp.arange(LANES, dtype=jnp.int32)[None, None, :]
    gates = jnp.sum(
        jnp.where(onehot, gate_weights.astype(jnp.float32)[:, :, None], 0.0), axis=1
    ).astype(jnp.bfloat16)
    own = jnp.concatenate([tokens, grad_out, gates], axis=1)

    arrived = [own] + [rotate(own, -k) for k in range(1, local_count)]
    order = [[0], [1, local_count - 1], list(range(2, local_count - 1))] if local_count > 2 else [[k] for k in range(local_count)]
    order = [g for g in order if g]
    mine, theirs = [], []
    for group in order:
        held = jnp.concatenate([arrived[k][None, None] for k in group], axis=0)
        for step in range(steps):
            held = jnp.concatenate([held, exchange(held, step)], axis=1)
        mine.append(held)
        theirs.append(sibling(held))
    spots = 1 << steps
    half = local_count * spots * tok_count
    rows = jnp.concatenate(
        [v.reshape(-1, v.shape[-1]) for v in mine] + [v.reshape(-1, v.shape[-1]) for v in theirs],
        axis=0,
    )
    flat_in = rows[:, :width]
    flat_grad = rows[:, width : 2 * width]
    me = lax.axis_index("node")
    lane = lax.broadcasted_iota(jnp.int32, (1, LANES), 1) == me
    flat_gate = jnp.sum(
        jnp.where(lane, rows[:, 2 * width :].astype(jnp.float32), 0.0), axis=1, keepdims=True
    )

    gate_proj, up_proj, down_proj = w_gate[0], w_up[0], w_down[0]
    gate_pre = jnp.dot(flat_in, gate_proj, preferred_element_type=jnp.float32)
    up_pre = jnp.dot(flat_in, up_proj, preferred_element_type=jnp.float32)
    sigmoid_val = jax.nn.sigmoid(gate_pre)
    activated = gate_pre * sigmoid_val
    slope = sigmoid_val * (1.0 + gate_pre * (1.0 - sigmoid_val))
    hidden = (activated * up_pre).astype(jnp.bfloat16)
    grad_hidden = lax.dot_general(
        flat_grad, down_proj, CONTRACT_COLS, preferred_element_type=jnp.float32
    )
    gate_partial = jnp.sum(hidden.astype(jnp.float32) * grad_hidden, axis=1, keepdims=True)
    scaled = flat_gate * grad_hidden
    grad_gate_pre = (scaled * up_pre * slope).astype(jnp.bfloat16)
    grad_up_pre = (scaled * activated).astype(jnp.bfloat16)
    weighted = (flat_gate * hidden.astype(jnp.float32)).astype(jnp.bfloat16)

    def returned(value):
        value = value.astype(jnp.bfloat16)
        total = value[:half].astype(jnp.float32) + sibling(value[half:]).astype(jnp.float32)
        total = total.reshape(local_count, spots, tok_count, -1)
        for step in reversed(range(steps)):
            keep = 1 << step
            sent = total[:, keep:].astype(jnp.bfloat16)
            total = total[:, :keep] + exchange(sent, step).astype(jnp.float32)
        total = total[:, 0].astype(jnp.bfloat16)
        places = [k for g in order for k in g]
        answer = total[0].astype(jnp.float32)
        for i in range(1, local_count):
            answer = answer + rotate(total[i], places[i]).astype(jnp.float32)
        return answer

    answers = []
    for chunk in range(CHUNKS):
        cols = slice(chunk * width // CHUNKS, (chunk + 1) * width // CHUNKS)
        part = lax.dot_general(
            grad_gate_pre, gate_proj[cols], CONTRACT_COLS, preferred_element_type=jnp.float32
        ) + lax.dot_general(
            grad_up_pre, up_proj[cols], CONTRACT_COLS, preferred_element_type=jnp.float32
        )
        if chunk == 0:
            part = jnp.concatenate([part, jnp.where(lane, gate_partial, 0.0)], axis=1)
        answers.append(returned(part))
    first = width // CHUNKS
    grad_in = jnp.concatenate([answers[0][:, :first]] + answers[1:], axis=1).astype(jnp.bfloat16)
    sums = answers[0][:, first:].astype(jnp.bfloat16).astype(jnp.float32)
    grad_gate = jnp.sum(jnp.where(onehot, sums[:, None, :], 0.0), axis=2).astype(jnp.bfloat16)

    grad_down = lax.dot_general(
        weighted, flat_grad, CONTRACT_ROWS, preferred_element_type=jnp.float32
    ).astype(jnp.bfloat16)
    grad_gate_w = lax.dot_general(
        flat_in, grad_gate_pre, CONTRACT_ROWS, preferred_element_type=jnp.float32
    ).astype(jnp.bfloat16)
    grad_up_w = lax.dot_general(
        flat_in, grad_up_pre, CONTRACT_ROWS, preferred_element_type=jnp.float32
    ).astype(jnp.bfloat16)
    return (grad_in, grad_gate, grad_gate_w[None], grad_up_w[None], grad_down[None])


def slotted(tokens, grad_out, expert_ids, gate_weights, w_gate, w_up, w_down):
    tok_count = tokens.shape[0]
    width = tokens.shape[1]
    top_count = expert_ids.shape[1]
    node_count = lax.axis_size("node")
    local_count = lax.axis_size("local")
    capacity = max(2, 2 * tok_count * top_count // node_count)
    onehot = (
        expert_ids[:, :, None] == jnp.arange(node_count, dtype=jnp.int32)[None, None, :]
    ).astype(jnp.int32)
    per_token = jnp.sum(onehot, axis=1)
    earlier = jnp.cumsum(per_token, axis=0) - per_token
    slot_index = jnp.sum(earlier[:, None, :] * onehot, axis=2)
    flat_slot = expert_ids * capacity + slot_index
    placing = (
        flat_slot[:, :, None] == jnp.arange(node_count * capacity, dtype=jnp.int32)[None, None, :]
    ).astype(jnp.float32)
    placing_tok = jnp.sum(placing, axis=1).astype(jnp.bfloat16)
    send_in = (
        jnp.dot(placing_tok.T, tokens, preferred_element_type=jnp.float32)
        .astype(jnp.bfloat16)
        .reshape(node_count, capacity, width)
    )
    send_grad = (
        jnp.dot(placing_tok.T, grad_out, preferred_element_type=jnp.float32)
        .astype(jnp.bfloat16)
        .reshape(node_count, capacity, width)
    )
    send_gate = (
        jnp.einsum(
            "tks,tk->s", placing, gate_weights.astype(jnp.float32), precision=lax.Precision.HIGHEST
        )
        .astype(jnp.bfloat16)
        .reshape(node_count, capacity)
    )
    recv_in, recv_grad, recv_gate = (
        lax.all_to_all(send_in, "node", split_axis=0, concat_axis=0, tiled=True),
        lax.all_to_all(send_grad, "node", split_axis=0, concat_axis=0, tiled=True),
        lax.all_to_all(send_gate, "node", split_axis=0, concat_axis=0, tiled=True),
    )
    rows_in, rows_grad, rows_gate = (
        lax.all_gather(recv_in[None], "local", axis=0, tiled=True),
        lax.all_gather(recv_grad[None], "local", axis=0, tiled=True),
        lax.all_gather(recv_gate[None], "local", axis=0, tiled=True),
    )
    rows_total = local_count * node_count * capacity
    flat_in = rows_in.reshape(rows_total, width)
    flat_grad = rows_grad.reshape(rows_total, width)
    flat_gate = rows_gate.reshape(rows_total).astype(jnp.float32)
    gate_proj = w_gate[0]
    up_proj = w_up[0]
    down_proj = w_down[0]
    contract_rows = (((0,), (0,)), ((), ()))
    contract_cols = (((1,), (1,)), ((), ()))
    gate_pre = jnp.dot(flat_in, gate_proj, preferred_element_type=jnp.float32)
    up_pre = jnp.dot(flat_in, up_proj, preferred_element_type=jnp.float32)
    sigmoid_val = jax.nn.sigmoid(gate_pre)
    activated = gate_pre * sigmoid_val
    slope = sigmoid_val * (1.0 + gate_pre * (1.0 - sigmoid_val))
    hidden = (activated * up_pre).astype(jnp.bfloat16)
    grad_hidden = lax.dot_general(
        flat_grad, down_proj, contract_cols, preferred_element_type=jnp.float32
    )
    gate_partial = jnp.sum(hidden.astype(jnp.float32) * grad_hidden, axis=1)
    scaled = flat_gate[:, None] * grad_hidden
    grad_gate_pre = (scaled * up_pre * slope).astype(jnp.bfloat16)
    grad_up_pre = (scaled * activated).astype(jnp.bfloat16)
    weighted = (flat_gate[:, None] * hidden.astype(jnp.float32)).astype(jnp.bfloat16)
    grad_down = lax.dot_general(
        weighted, flat_grad, contract_rows, preferred_element_type=jnp.float32
    ).astype(jnp.bfloat16)
    grad_gate_w = lax.dot_general(
        flat_in, grad_gate_pre, contract_rows, preferred_element_type=jnp.float32
    ).astype(jnp.bfloat16)
    grad_up_w = lax.dot_general(
        flat_in, grad_up_pre, contract_rows, preferred_element_type=jnp.float32
    ).astype(jnp.bfloat16)
    input_partial = lax.dot_general(
        grad_gate_pre, gate_proj, contract_cols, preferred_element_type=jnp.float32
    )
    input_partial = input_partial + lax.dot_general(
        grad_up_pre, up_proj, contract_cols, preferred_element_type=jnp.float32
    )
    input_blocks = input_partial.reshape(local_count, node_count, capacity, width)
    gate_blocks = gate_partial.reshape(local_count, node_count, capacity)
    summed_in, summed_gate = (
        lax.psum_scatter(
            input_blocks.astype(jnp.bfloat16), "local", scatter_dimension=0, tiled=True
        ).astype(jnp.float32),
        lax.psum_scatter(
            gate_blocks.astype(jnp.bfloat16), "local", scatter_dimension=0, tiled=True
        ).astype(jnp.float32),
    )
    back_in, back_gate = (
        lax.all_to_all(
            summed_in[0].astype(jnp.bfloat16), "node", split_axis=0, concat_axis=0, tiled=True
        ),
        lax.all_to_all(
            summed_gate[0].astype(jnp.bfloat16), "node", split_axis=0, concat_axis=0, tiled=True
        ),
    )
    grad_in = jnp.dot(
        placing_tok,
        back_in.reshape(node_count * capacity, width),
        preferred_element_type=jnp.float32,
    ).astype(jnp.bfloat16)
    grad_gate = jnp.einsum(
        "tks,s->tk",
        placing,
        back_gate.reshape(node_count * capacity).astype(jnp.float32),
        precision=lax.Precision.HIGHEST,
    ).astype(jnp.bfloat16)
    return (grad_in, grad_gate, grad_gate_w[None], grad_up_w[None], grad_down[None])


def per_device(tokens, grad_out, expert_ids, gate_weights, w_gate, w_up, w_down):
    tok_count, top_count = expert_ids.shape
    node_count = lax.axis_size("node")
    capacity = max(2, 2 * tok_count * top_count // node_count)
    paired = node_count & (node_count - 1) == 0 and 1 < node_count <= LANES
    plan = dense if capacity >= tok_count and paired else slotted
    return plan(tokens, grad_out, expert_ids, gate_weights, w_gate, w_up, w_down)


def solution(mesh):
    placed = (
        P(("node", "local"), None),
        P(("node", "local"), None),
        P(("node", "local"), None),
        P(("node", "local"), None),
        P("node", None, "local"),
        P("node", None, "local"),
        P("node", "local", None),
    )
    return jax.shard_map(
        per_device,
        mesh=mesh,
        in_specs=placed,
        out_specs=(
            P(("node", "local"), None),
            P(("node", "local"), None),
            P("node", None, "local"),
            P("node", None, "local"),
            P("node", "local", None),
        ),
        check_vma=False,
    )
```

```python
import functools

import jax
import jax.numpy as jnp
from jax import lax
from jax.experimental import pallas as pl
from jax.experimental.pallas import tpu as pltpu
from jax.sharding import PartitionSpec as P

AXES = ("node", "local")
LANES = 128
NO_COST = pl.CostEstimate(flops=0, bytes_accessed=0, transcendentals=0)
CONTRACT_ROWS = (((0,), (0,)), ((), ()))
CONTRACT_COLS = (((1,), (1,)), ((), ()))


def whole(count):
    return (pl.BlockSpec(memory_space=pltpu.VMEM),) * count


def in_hbm(value):
    return pltpu.with_memory_space_constraint(value, pltpu.HBM)


def pack_kernel(
    tokens_hbm, grad_hbm, ids_hbm, gates_hbm, own_ref, ids_ref, gates_ref, square, sems
):
    width = tokens_hbm.shape[1]
    pairs = (
        (ids_hbm, ids_ref),
        (gates_hbm, gates_ref),
        (tokens_hbm, own_ref.at[:, pl.ds(0, width)]),
        (grad_hbm, own_ref.at[:, pl.ds(width, width)]),
    )
    copies = [pltpu.make_async_copy(*pair, sems.at[i]) for i, pair in enumerate(pairs)]
    for copy in copies:
        copy.start()
    copies[0].wait()
    copies[1].wait()
    ids, gates = ids_ref[...], gates_ref[...].astype(jnp.float32)
    top_count, tok_count = ids.shape
    experts = lax.broadcasted_iota(jnp.int32, (LANES, tok_count), 0)
    table = jnp.zeros(experts.shape, jnp.float32)
    for k in range(top_count):
        table = table + jnp.where(experts == ids[k : k + 1], gates[k : k + 1], 0.0)
    square[...] = jnp.zeros(square.shape, jnp.float32)
    square[:, :tok_count] = table
    own_ref[:, 2 * width :] = square[...].T[:tok_count].astype(jnp.bfloat16)
    copies[2].wait()
    copies[3].wait()


def pack(tokens, grad_out, expert_ids, gate_weights):
    rows, width = tokens.shape
    hbm = pl.BlockSpec(memory_space=pl.ANY)
    return pl.pallas_call(
        pack_kernel,
        out_shape=jax.ShapeDtypeStruct((rows, 2 * width + LANES), tokens.dtype),
        in_specs=[hbm] * 4,
        out_specs=whole(1)[0],
        scratch_shapes=[
            pltpu.VMEM(expert_ids.T.shape, expert_ids.dtype),
            pltpu.VMEM(gate_weights.T.shape, gate_weights.dtype),
            pltpu.VMEM((LANES, LANES), jnp.float32),
            pltpu.SemaphoreType.DMA((4,)),
        ],
        compiler_params=pltpu.CompilerParams(vmem_limit_bytes=4 << 20),
        cost_estimate=NO_COST,
    )(*(in_hbm(v) for v in (tokens, grad_out, expert_ids.T, gate_weights.T)))


def finish_kernel(*refs):
    *terms, ids_ref, rows_ref, gates_ref, square = refs
    width = rows_ref.shape[1]
    total = terms[0][...].astype(jnp.float32)
    for term in terms[1:]:
        total = total + term[...].astype(jnp.float32)
    rows_ref[...] = total[:, :width].astype(jnp.bfloat16)
    ids = ids_ref[...]
    top_count, tok_count = ids.shape
    square[...] = jnp.zeros(square.shape, jnp.float32)
    square[:tok_count] = total[:, width:].astype(jnp.bfloat16).astype(jnp.float32)
    sums = square[...].T[:, :tok_count]
    experts = lax.broadcasted_iota(jnp.int32, sums.shape, 0)
    slots = lax.broadcasted_iota(jnp.int32, ids.shape, 0)
    picked = jnp.zeros(ids.shape, jnp.float32)
    for k in range(top_count):
        value = jnp.sum(jnp.where(experts == ids[k : k + 1], sums, 0.0), axis=0, keepdims=True)
        picked = picked + jnp.where(slots == k, value, 0.0)
    gates_ref[...] = picked.astype(jnp.bfloat16)


def finish(terms, expert_ids):
    rows, columns = terms[0].shape
    ids = expert_ids.T
    grad_in, grad_gate = pl.pallas_call(
        finish_kernel,
        out_shape=(
            jax.ShapeDtypeStruct((rows, columns - LANES), jnp.bfloat16),
            jax.ShapeDtypeStruct(ids.shape, jnp.bfloat16),
        ),
        in_specs=list(whole(len(terms) + 1)),
        out_specs=whole(2),
        scratch_shapes=[pltpu.VMEM((LANES, LANES), jnp.float32)],
        compiler_params=pltpu.CompilerParams(vmem_limit_bytes=4 << 20),
        cost_estimate=NO_COST,
    )(*terms, ids)
    return grad_in, grad_gate.T


def weights_kernel(*refs, blocks, groups, width, chunk):
    rows, refs = refs[:blocks], refs[blocks:]
    da, du, hw, refs = refs[:groups], refs[groups : 2 * groups], refs[2 * groups : 3 * groups], refs[3 * groups :]
    outs, parts, sems = refs[:3], refs[3:6], refs[6]

    def stacked(pieces, span=slice(None)):
        return jnp.concatenate([p[:, span] for p in pieces], axis=0)

    def outer(left, right):
        product = lax.dot_general(left, right, CONTRACT_ROWS, preferred_element_type=jnp.float32)
        return product.astype(jnp.bfloat16)

    gate_side, up_side, down_side = stacked(da), stacked(du), stacked(hw)
    copies = []
    for c in range(width // chunk):
        span = pl.ds(c * chunk, chunk)
        part_in = stacked(rows, span)
        parts[0][span, :] = outer(part_in, gate_side)
        parts[1][span, :] = outer(part_in, up_side)
        parts[2][:, span] = outer(down_side, stacked(rows, pl.ds(width + c * chunk, chunk)))
        places = ((span, slice(None)), (span, slice(None)), (slice(None), span))
        for i, place in enumerate(places):
            copies.append(pltpu.make_async_copy(parts[i].at[place], outs[i].at[place], sems.at[i, c]))
            copies[-1].start()
    for copy in copies:
        copy.wait()


def weight_terms(rows, da, du, hw, width):
    hid = da[0].shape[1]
    chunk = next(c for c in (1024, 512, 256, 128) if width % c == 0)
    shapes = ((width, hid), (width, hid), (hid, width))
    hbm = pl.BlockSpec(memory_space=pl.ANY)
    return pl.pallas_call(
        functools.partial(
            weights_kernel, blocks=len(rows), groups=len(da), width=width, chunk=chunk
        ),
        out_shape=tuple(jax.ShapeDtypeStruct(s, jnp.bfloat16) for s in shapes),
        in_specs=list(whole(len(rows) + 3 * len(da))),
        out_specs=(hbm,) * 3,
        scratch_shapes=[
            *(pltpu.VMEM(s, jnp.bfloat16) for s in shapes),
            pltpu.SemaphoreType.DMA((3, width // chunk)),
        ],
        compiler_params=pltpu.CompilerParams(vmem_limit_bytes=28 << 20),
        cost_estimate=NO_COST,
    )(*rows, *da, *du, *hw)


def in_vmem(value):
    return pltpu.with_memory_space_constraint(value, pltpu.VMEM)


def group_kernel(*refs, width, chunk, loads):
    me_ref, held_ref, other_ref = refs[:3]
    sources, refs = refs[3:6], refs[6:]
    mine_ref, send_ref, da_ref, du_ref, hw_ref = refs[:5]
    spans = [pl.ds(c * chunk, chunk) for c in range(width // chunk)]
    copies = [[] for _ in spans]
    gate_w, up_w, down_w = refs[5:8] if loads else sources
    if loads:
        sems = refs[8]
        for c, span in enumerate(spans):
            places = ((span, slice(None)), (span, slice(None)), (slice(None), span))
            for i, place in enumerate(places):
                copies[c].append(
                    pltpu.make_async_copy(sources[i].at[place], refs[5 + i].at[place], sems.at[i, c])
                )
                copies[c][-1].start()
    half = held_ref.shape[0]

    def rows(start, size):
        span = pl.ds(start, size)
        return jnp.concatenate([held_ref[:, span], other_ref[:, span]], axis=0)

    extra = rows(2 * width, LANES).astype(jnp.float32)
    named = lax.broadcasted_iota(jnp.int32, extra.shape, 1) == me_ref[0]
    flat_gate = jnp.sum(jnp.where(named, extra, 0.0), axis=1, keepdims=True)

    def plain(a, b):
        return lax.dot_general(a, b, (((1,), (0,)), ((), ())), preferred_element_type=jnp.float32)

    def turned(a, b):
        return lax.dot_general(a, b, CONTRACT_COLS, preferred_element_type=jnp.float32)

    gate_pre = up_pre = grad_hidden = 0.0
    for c, span in enumerate(spans):
        for copy in copies[c]:
            copy.wait()
        part_in = rows(c * chunk, chunk)
        gate_pre += plain(part_in, gate_w[span, :])
        up_pre += plain(part_in, up_w[span, :])
        grad_hidden += turned(rows(width + c * chunk, chunk), down_w[:, span])
    sigmoid_val = jax.nn.sigmoid(gate_pre)
    activated = gate_pre * sigmoid_val
    slope = sigmoid_val * (1.0 + gate_pre * (1.0 - sigmoid_val))
    hidden = (activated * up_pre).astype(jnp.bfloat16).astype(jnp.float32)
    gate_partial = jnp.sum(hidden * grad_hidden, axis=1, keepdims=True)
    scaled = flat_gate * grad_hidden
    grad_gate_pre = (scaled * up_pre * slope).astype(jnp.bfloat16)
    grad_up_pre = (scaled * activated).astype(jnp.bfloat16)
    da_ref[...] = grad_gate_pre
    du_ref[...] = grad_up_pre
    hw_ref[...] = (flat_gate * hidden).astype(jnp.bfloat16)
    for span in spans:
        part = turned(grad_gate_pre, gate_w[span, :]) + turned(grad_up_pre, up_w[span, :])
        part = part.astype(jnp.bfloat16)
        mine_ref[:, span] = part[:half]
        send_ref[:, span] = part[half:]
    gate_term = jnp.where(named, gate_partial, 0.0).astype(jnp.bfloat16)
    last = pl.ds(width, LANES)
    mine_ref[:, last] = gate_term[:half]
    send_ref[:, last] = gate_term[half:]


def group_terms(held, other, weights, loads):
    count, columns = held.shape
    width, hid = weights[0].shape
    chunk = next(c for c in (1024, 512, 256, 128) if width % c == 0)
    me = lax.axis_index("node").astype(jnp.int32).reshape(1)
    back = jax.ShapeDtypeStruct((count, width + LANES), jnp.bfloat16)
    unit = jax.ShapeDtypeStruct((2 * count, hid), jnp.bfloat16)
    shapes = (back, back, unit, unit, unit)
    if loads:
        shapes += tuple(pltpu.VMEM(w.shape, w.dtype) for w in weights)
    space = pl.ANY if loads else pltpu.VMEM
    place = in_hbm if loads else in_vmem
    *terms, = pl.pallas_call(
        functools.partial(group_kernel, width=width, chunk=chunk, loads=loads),
        out_shape=shapes,
        in_specs=[
            pl.BlockSpec(memory_space=pltpu.SMEM),
            *whole(2),
            *(pl.BlockSpec(memory_space=space),) * 3,
        ],
        out_specs=whole(len(shapes)),
        scratch_shapes=[pltpu.SemaphoreType.DMA((3, width // chunk))] if loads else [],
        compiler_params=pltpu.CompilerParams(vmem_limit_bytes=16 << 20),
        cost_estimate=NO_COST,
    )(me, held, other, *(place(w) for w in weights))
    return terms[:5], terms[5:]


def dense(tokens, grad_out, expert_ids, gate_weights, w_gate, w_up, w_down):
    tok_count, width = tokens.shape
    node_count = lax.axis_size("node")
    local_count = lax.axis_size("local")
    clock = []

    def tick(*values):
        held = lax.optimization_barrier((*values, *clock))[: len(values)]
        return held[0] if len(values) == 1 else held

    def tock(value):
        clock[:] = [value]
        return value

    def permute(value, target):
        pairs = []
        for node in range(node_count):
            for place in range(local_count):
                to_node, to_place = target(node, place)
                pairs.append((node * local_count + place, to_node * local_count + to_place))
        return lax.ppermute(value, AXES, pairs)

    def cross(value, step):
        return permute(value, lambda n, p: (n ^ (2 if (n % 2 == 0) == (step == 0) else 4), p))

    def sibling(value):
        return permute(value, lambda n, p: (n ^ 1, p))

    def rotate(value, k):
        return permute(value, lambda n, p: (n, (p + k) % local_count))

    def joined(*values):
        return jnp.concatenate(values, axis=1)

    own = pack(tokens, grad_out, expert_ids, gate_weights)[None, None]

    weights = (w_gate[0], w_up[0], w_down[0])

    def terms(held, other, weights, loads):
        flat = [v.reshape(-1, v.shape[-1]) for v in (held, other)]
        return group_terms(*flat, weights, loads)

    def summed(mine, received):
        total = mine.astype(jnp.float32) + received.astype(jnp.float32)
        return total.reshape(-1, 4, tok_count, total.shape[-1]).astype(jnp.bfloat16)

    def folded(total, received):
        keep = received.shape[1]
        return (total[:, :keep].astype(jnp.float32) + received.astype(jnp.float32)).astype(jnp.bfloat16)

    def upper(total):
        return total[:, total.shape[1] // 2 :]


    weights = (w_gate[0], w_up[0], w_down[0])
    near_x = cross(own, 0)
    up_in = rotate(own, -1)
    down_in = rotate(own, 1)
    near = tock(joined(*tick(own, near_x)))
    near_y = cross(near, 1)
    up = tock(tick(up_in))
    up_x = cross(up, 0)
    far_in = rotate(up, -1)
    down = tock(tick(down_in))
    down_x = cross(down, 0)
    up = tock(joined(*tick(up, up_x)))
    up_y = cross(up, 1)
    far = tock(tick(far_in))
    far_x = cross(far, 0)
    down = tock(joined(*tick(down, down_x)))
    down_y = cross(down, 1)
    up = tock(joined(*tick(up, up_y)))
    near = tock(joined(*tick(near, near_y)))
    first = tock(jnp.concatenate(tick(near, up), axis=0))
    first_other = sibling(first)
    far = tock(joined(*tick(far, far_x)))
    far_y = cross(far, 1)
    down = tock(joined(*tick(down, down_y)))
    first_terms, weights = terms(*tick(first, first_other), weights, True)
    tock(first_terms[0])
    first_back = sibling(first_terms[1])
    far = tock(joined(*tick(far, far_y)))
    second = tock(jnp.concatenate(tick(down, far), axis=0))
    second_other = sibling(second)
    first_sum = tock(summed(*tick(first_terms[0], first_back)))
    first_r1 = cross(upper(first_sum), 1)
    second_terms, _ = terms(*tick(second, second_other), weights, False)
    tock(second_terms[0])
    second_back = sibling(second_terms[1])
    first_sum = tock(folded(*tick(first_sum, first_r1)))
    first_r2 = cross(upper(first_sum), 0)
    second_sum = tock(summed(*tick(second_terms[0], second_back)))
    second_r1 = cross(upper(second_sum), 1)
    first_sum = tock(folded(*tick(first_sum, first_r2)))
    from_up = rotate(first_sum[1], 1)
    second_sum = tock(folded(*tick(second_sum, second_r1)))
    second_r2 = cross(upper(second_sum), 0)
    from_up = tock(tick(from_up))
    second_sum = tock(folded(*tick(second_sum, second_r2)))
    from_down = rotate(second_sum[0], -1)
    from_far = rotate(second_sum[1], 2)
    rows = [v.reshape(-1, v.shape[-1]) for v in (first, first_other, second, second_other)]
    rows[0] = tick(rows[0])
    sides = [[t[i] for t in (first_terms, second_terms)] for i in (2, 3, 4)]
    grad_gate_w, grad_up_w, grad_down = weight_terms(rows, *sides, width)
    tock(grad_down)
    ends = tick(first_sum[0], from_up, from_down, from_far)
    grad_in, grad_gate = finish([e[0] for e in ends], expert_ids)
    return (grad_in, grad_gate, grad_gate_w[None], grad_up_w[None], grad_down[None])


def slotted(tokens, grad_out, expert_ids, gate_weights, w_gate, w_up, w_down):
    tok_count = tokens.shape[0]
    width = tokens.shape[1]
    top_count = expert_ids.shape[1]
    node_count = lax.axis_size("node")
    local_count = lax.axis_size("local")
    capacity = max(2, 2 * tok_count * top_count // node_count)
    onehot = (
        expert_ids[:, :, None] == jnp.arange(node_count, dtype=jnp.int32)[None, None, :]
    ).astype(jnp.int32)
    per_token = jnp.sum(onehot, axis=1)
    earlier = jnp.cumsum(per_token, axis=0) - per_token
    slot_index = jnp.sum(earlier[:, None, :] * onehot, axis=2)
    flat_slot = expert_ids * capacity + slot_index
    placing = (
        flat_slot[:, :, None] == jnp.arange(node_count * capacity, dtype=jnp.int32)[None, None, :]
    ).astype(jnp.float32)
    placing_tok = jnp.sum(placing, axis=1).astype(jnp.bfloat16)
    send_in = (
        jnp.dot(placing_tok.T, tokens, preferred_element_type=jnp.float32)
        .astype(jnp.bfloat16)
        .reshape(node_count, capacity, width)
    )
    send_grad = (
        jnp.dot(placing_tok.T, grad_out, preferred_element_type=jnp.float32)
        .astype(jnp.bfloat16)
        .reshape(node_count, capacity, width)
    )
    send_gate = (
        jnp.einsum(
            "tks,tk->s", placing, gate_weights.astype(jnp.float32), precision=lax.Precision.HIGHEST
        )
        .astype(jnp.bfloat16)
        .reshape(node_count, capacity)
    )
    recv_in, recv_grad, recv_gate = (
        lax.all_to_all(send_in, "node", split_axis=0, concat_axis=0, tiled=True),
        lax.all_to_all(send_grad, "node", split_axis=0, concat_axis=0, tiled=True),
        lax.all_to_all(send_gate, "node", split_axis=0, concat_axis=0, tiled=True),
    )
    rows_in, rows_grad, rows_gate = (
        lax.all_gather(recv_in[None], "local", axis=0, tiled=True),
        lax.all_gather(recv_grad[None], "local", axis=0, tiled=True),
        lax.all_gather(recv_gate[None], "local", axis=0, tiled=True),
    )
    rows_total = local_count * node_count * capacity
    flat_in = rows_in.reshape(rows_total, width)
    flat_grad = rows_grad.reshape(rows_total, width)
    flat_gate = rows_gate.reshape(rows_total).astype(jnp.float32)
    gate_proj = w_gate[0]
    up_proj = w_up[0]
    down_proj = w_down[0]
    contract_rows = (((0,), (0,)), ((), ()))
    contract_cols = (((1,), (1,)), ((), ()))
    gate_pre = jnp.dot(flat_in, gate_proj, preferred_element_type=jnp.float32)
    up_pre = jnp.dot(flat_in, up_proj, preferred_element_type=jnp.float32)
    sigmoid_val = jax.nn.sigmoid(gate_pre)
    activated = gate_pre * sigmoid_val
    slope = sigmoid_val * (1.0 + gate_pre * (1.0 - sigmoid_val))
    hidden = (activated * up_pre).astype(jnp.bfloat16)
    grad_hidden = lax.dot_general(
        flat_grad, down_proj, contract_cols, preferred_element_type=jnp.float32
    )
    gate_partial = jnp.sum(hidden.astype(jnp.float32) * grad_hidden, axis=1)
    scaled = flat_gate[:, None] * grad_hidden
    grad_gate_pre = (scaled * up_pre * slope).astype(jnp.bfloat16)
    grad_up_pre = (scaled * activated).astype(jnp.bfloat16)
    weighted = (flat_gate[:, None] * hidden.astype(jnp.float32)).astype(jnp.bfloat16)
    grad_down = lax.dot_general(
        weighted, flat_grad, contract_rows, preferred_element_type=jnp.float32
    ).astype(jnp.bfloat16)
    grad_gate_w = lax.dot_general(
        flat_in, grad_gate_pre, contract_rows, preferred_element_type=jnp.float32
    ).astype(jnp.bfloat16)
    grad_up_w = lax.dot_general(
        flat_in, grad_up_pre, contract_rows, preferred_element_type=jnp.float32
    ).astype(jnp.bfloat16)
    input_partial = lax.dot_general(
        grad_gate_pre, gate_proj, contract_cols, preferred_element_type=jnp.float32
    )
    input_partial = input_partial + lax.dot_general(
        grad_up_pre, up_proj, contract_cols, preferred_element_type=jnp.float32
    )
    input_blocks = input_partial.reshape(local_count, node_count, capacity, width)
    gate_blocks = gate_partial.reshape(local_count, node_count, capacity)
    summed_in, summed_gate = (
        lax.psum_scatter(
            input_blocks.astype(jnp.bfloat16), "local", scatter_dimension=0, tiled=True
        ).astype(jnp.float32),
        lax.psum_scatter(
            gate_blocks.astype(jnp.bfloat16), "local", scatter_dimension=0, tiled=True
        ).astype(jnp.float32),
    )
    back_in, back_gate = (
        lax.all_to_all(
            summed_in[0].astype(jnp.bfloat16), "node", split_axis=0, concat_axis=0, tiled=True
        ),
        lax.all_to_all(
            summed_gate[0].astype(jnp.bfloat16), "node", split_axis=0, concat_axis=0, tiled=True
        ),
    )
    grad_in = jnp.dot(
        placing_tok,
        back_in.reshape(node_count * capacity, width),
        preferred_element_type=jnp.float32,
    ).astype(jnp.bfloat16)
    grad_gate = jnp.einsum(
        "tks,s->tk",
        placing,
        back_gate.reshape(node_count * capacity).astype(jnp.float32),
        precision=lax.Precision.HIGHEST,
    ).astype(jnp.bfloat16)
    return (grad_in, grad_gate, grad_gate_w[None], grad_up_w[None], grad_down[None])


def per_device(tokens, grad_out, expert_ids, gate_weights, w_gate, w_up, w_down):
    tok_count, top_count = expert_ids.shape
    node_count = lax.axis_size("node")
    capacity = max(2, 2 * tok_count * top_count // node_count)
    paired = node_count == 8 and lax.axis_size("local") == 4
    plan = dense if capacity >= tok_count and paired else slotted
    return plan(tokens, grad_out, expert_ids, gate_weights, w_gate, w_up, w_down)


def solution(mesh):
    placed = (
        P(("node", "local"), None),
        P(("node", "local"), None),
        P(("node", "local"), None),
        P(("node", "local"), None),
        P("node", None, "local"),
        P("node", None, "local"),
        P("node", "local", None),
    )
    return jax.shard_map(
        per_device,
        mesh=mesh,
        in_specs=placed,
        out_specs=(
            P(("node", "local"), None),
            P(("node", "local"), None),
            P("node", None, "local"),
            P("node", None, "local"),
            P("node", "local", None),
        ),
        check_vma=False,
    )
```

```python
import functools

import jax
import jax.numpy as jnp
from jax import lax
from jax.experimental import pallas as pl
from jax.experimental.pallas import tpu as pltpu
from jax.sharding import PartitionSpec as P

AXES = ("node", "local")
LANES = 128
NO_COST = pl.CostEstimate(flops=0, bytes_accessed=0, transcendentals=0)
CONTRACT_ROWS = (((0,), (0,)), ((), ()))
CONTRACT_COLS = (((1,), (1,)), ((), ()))


def whole(count):
    return (pl.BlockSpec(memory_space=pltpu.VMEM),) * count


def in_hbm(value):
    return pltpu.with_memory_space_constraint(value, pltpu.HBM)


def load_kernel(*refs):
    *refs, sems = refs
    count = len(refs) // 2
    copies = [pltpu.make_async_copy(refs[i], refs[count + i], sems.at[i]) for i in range(count)]
    for copy in copies:
        copy.start()
    for copy in copies:
        copy.wait()


def load(*values):
    return pl.pallas_call(
        load_kernel,
        out_shape=tuple(pltpu.VMEM(v.shape, v.dtype) for v in values),
        in_specs=[pl.BlockSpec(memory_space=pl.ANY)] * len(values),
        out_specs=whole(len(values)),
        scratch_shapes=[pltpu.SemaphoreType.DMA((len(values),))],
        compiler_params=pltpu.CompilerParams(vmem_limit_bytes=1 << 20),
        cost_estimate=NO_COST,
    )(*(in_hbm(v) for v in values))


def pack_kernel(
    tokens_hbm, grad_hbm, ids_hbm, gates_hbm, own_ref, ids_ref, gates_ref, square, sems
):
    width = tokens_hbm.shape[1]
    pairs = (
        (ids_hbm, ids_ref),
        (gates_hbm, gates_ref),
        (tokens_hbm, own_ref.at[:, pl.ds(0, width)]),
        (grad_hbm, own_ref.at[:, pl.ds(width, width)]),
    )
    copies = [pltpu.make_async_copy(*pair, sems.at[i]) for i, pair in enumerate(pairs)]
    for copy in copies:
        copy.start()
    copies[0].wait()
    copies[1].wait()
    ids, gates = ids_ref[...], gates_ref[...].astype(jnp.float32)
    top_count, tok_count = ids.shape
    experts = lax.broadcasted_iota(jnp.int32, (LANES, tok_count), 0)
    table = jnp.zeros(experts.shape, jnp.float32)
    for k in range(top_count):
        table = table + jnp.where(experts == ids[k : k + 1], gates[k : k + 1], 0.0)
    square[...] = jnp.zeros(square.shape, jnp.float32)
    square[:, :tok_count] = table
    own_ref[:, 2 * width :] = square[...].T[:tok_count].astype(jnp.bfloat16)
    copies[2].wait()
    copies[3].wait()


def pack(tokens, grad_out, expert_ids, gate_weights):
    rows, width = tokens.shape
    hbm = pl.BlockSpec(memory_space=pl.ANY)
    return pl.pallas_call(
        pack_kernel,
        out_shape=jax.ShapeDtypeStruct((rows, 2 * width + LANES), tokens.dtype),
        in_specs=[hbm] * 4,
        out_specs=whole(1)[0],
        scratch_shapes=[
            pltpu.VMEM(expert_ids.T.shape, expert_ids.dtype),
            pltpu.VMEM(gate_weights.T.shape, gate_weights.dtype),
            pltpu.VMEM((LANES, LANES), jnp.float32),
            pltpu.SemaphoreType.DMA((4,)),
        ],
        compiler_params=pltpu.CompilerParams(vmem_limit_bytes=2 << 20),
        cost_estimate=NO_COST,
    )(*(in_hbm(v) for v in (tokens, grad_out, expert_ids.T, gate_weights.T)))


def finish_kernel(*refs):
    *terms, ids_ref, rows_ref, gates_ref, square = refs
    width = rows_ref.shape[1]
    total = terms[0][...].astype(jnp.float32)
    for term in terms[1:]:
        total = total + term[...].astype(jnp.float32)
    rows_ref[...] = total[:, :width].astype(jnp.bfloat16)
    ids = ids_ref[...]
    top_count, tok_count = ids.shape
    square[...] = jnp.zeros(square.shape, jnp.float32)
    square[:tok_count] = total[:, width:].astype(jnp.bfloat16).astype(jnp.float32)
    sums = square[...].T[:, :tok_count]
    experts = lax.broadcasted_iota(jnp.int32, sums.shape, 0)
    slots = lax.broadcasted_iota(jnp.int32, ids.shape, 0)
    picked = jnp.zeros(ids.shape, jnp.float32)
    for k in range(top_count):
        value = jnp.sum(jnp.where(experts == ids[k : k + 1], sums, 0.0), axis=0, keepdims=True)
        picked = picked + jnp.where(slots == k, value, 0.0)
    gates_ref[...] = picked.astype(jnp.bfloat16)


def finish(terms, expert_ids):
    rows, columns = terms[0].shape
    ids = expert_ids.T
    grad_in, grad_gate = pl.pallas_call(
        finish_kernel,
        out_shape=(
            jax.ShapeDtypeStruct((rows, columns - LANES), jnp.bfloat16),
            jax.ShapeDtypeStruct(ids.shape, jnp.bfloat16),
        ),
        in_specs=list(whole(len(terms) + 1)),
        out_specs=whole(2),
        scratch_shapes=[pltpu.VMEM((LANES, LANES), jnp.float32)],
        compiler_params=pltpu.CompilerParams(vmem_limit_bytes=2 << 20),
        cost_estimate=NO_COST,
    )(*terms, ids)
    return grad_in, grad_gate.T


def weights_kernel(*refs, blocks, groups, width, chunk):
    rows, refs = refs[:blocks], refs[blocks:]
    da, du, hw, refs = refs[:groups], refs[groups : 2 * groups], refs[2 * groups : 3 * groups], refs[3 * groups :]
    outs, parts, sems = refs[:3], refs[3:6], refs[6]

    def stacked(pieces, span=slice(None)):
        return jnp.concatenate([p[:, span] for p in pieces], axis=0)

    def outer(left, right):
        product = lax.dot_general(left, right, CONTRACT_ROWS, preferred_element_type=jnp.float32)
        return product.astype(jnp.bfloat16)

    gate_side, up_side, down_side = stacked(da), stacked(du), stacked(hw)
    copies = []
    for c in range(width // chunk):
        slot, span = c % 2, pl.ds(c * chunk, chunk)
        for copy in copies[c - 2] if c > 1 else ():
            copy.wait()
        part_in = stacked(rows, span)
        parts[0][slot] = outer(part_in, gate_side)
        parts[1][slot] = outer(part_in, up_side)
        parts[2][slot] = outer(down_side, stacked(rows, pl.ds(width + c * chunk, chunk)))
        places = ((span, slice(None)), (span, slice(None)), (slice(None), span))
        copies.append(
            [
                pltpu.make_async_copy(parts[i].at[slot], outs[i].at[place], sems.at[i, slot])
                for i, place in enumerate(places)
            ]
        )
        for copy in copies[-1]:
            copy.start()
    for copy in sum(copies[-2:], []):
        copy.wait()


def weight_terms(rows, da, du, hw, width):
    hid = da[0].shape[1]
    chunk = next(c for c in (1024, 512, 256, 128) if width % c == 0)
    shapes = ((width, hid), (width, hid), (hid, width))
    hbm = pl.BlockSpec(memory_space=pl.ANY)
    return pl.pallas_call(
        functools.partial(
            weights_kernel, blocks=len(rows), groups=len(da), width=width, chunk=chunk
        ),
        out_shape=tuple(jax.ShapeDtypeStruct(s, jnp.bfloat16) for s in shapes),
        in_specs=list(whole(len(rows) + 3 * len(da))),
        out_specs=(hbm,) * 3,
        scratch_shapes=[
            pltpu.VMEM((2, chunk, hid), jnp.bfloat16),
            pltpu.VMEM((2, chunk, hid), jnp.bfloat16),
            pltpu.VMEM((2, hid, chunk), jnp.bfloat16),
            pltpu.SemaphoreType.DMA((3, 2)),
        ],
        compiler_params=pltpu.CompilerParams(vmem_limit_bytes=10 << 20),
        cost_estimate=pl.CostEstimate(
            flops=0, bytes_accessed=16 << 18, transcendentals=0
        ),
    )(*rows, *da, *du, *hw)


def in_vmem(value):
    return pltpu.with_memory_space_constraint(value, pltpu.VMEM)


def hidden_kernel(*refs, width, chunk, loads):
    me_ref, held_ref, other_ref = refs[:3]
    sources, refs = refs[3:6], refs[6:]
    da_ref, du_ref, hw_ref, term_ref = refs[:4]
    spans = [pl.ds(c * chunk, chunk) for c in range(width // chunk)]
    copies = [[] for _ in spans]
    gate_w, up_w, down_w = refs[4:7] if loads else sources
    if loads:
        sems = refs[7]
        for c, span in enumerate(spans):
            places = ((span, slice(None)), (span, slice(None)), (slice(None), span))
            for i, place in enumerate(places):
                copies[c].append(
                    pltpu.make_async_copy(sources[i].at[place], refs[4 + i].at[place], sems.at[i, c])
                )
                copies[c][-1].start()

    def rows(start, size):
        span = pl.ds(start, size)
        return jnp.concatenate([held_ref[:, span], other_ref[:, span]], axis=0)

    extra = rows(2 * width, LANES).astype(jnp.float32)
    named = lax.broadcasted_iota(jnp.int32, extra.shape, 1) == me_ref[0]
    flat_gate = jnp.sum(jnp.where(named, extra, 0.0), axis=1, keepdims=True)

    def plain(a, b):
        return lax.dot_general(a, b, (((1,), (0,)), ((), ())), preferred_element_type=jnp.float32)

    def turned(a, b):
        return lax.dot_general(a, b, CONTRACT_COLS, preferred_element_type=jnp.float32)

    gate_pre = up_pre = grad_hidden = 0.0
    for c, span in enumerate(spans):
        for copy in copies[c]:
            copy.wait()
        part_in = rows(c * chunk, chunk)
        gate_pre += plain(part_in, gate_w[span, :])
        up_pre += plain(part_in, up_w[span, :])
        grad_hidden += turned(rows(width + c * chunk, chunk), down_w[:, span])
    sigmoid_val = jax.nn.sigmoid(gate_pre)
    activated = gate_pre * sigmoid_val
    slope = sigmoid_val * (1.0 + gate_pre * (1.0 - sigmoid_val))
    hidden = (activated * up_pre).astype(jnp.bfloat16).astype(jnp.float32)
    gate_partial = jnp.sum(hidden * grad_hidden, axis=1, keepdims=True)
    scaled = flat_gate * grad_hidden
    grad_gate_pre = (scaled * up_pre * slope).astype(jnp.bfloat16)
    grad_up_pre = (scaled * activated).astype(jnp.bfloat16)
    da_ref[...] = grad_gate_pre
    du_ref[...] = grad_up_pre
    hw_ref[...] = (flat_gate * hidden).astype(jnp.bfloat16)
    term_ref[...] = jnp.where(named, gate_partial, 0.0).astype(jnp.bfloat16)


def rows_kernel(da_ref, du_ref, term_ref, gate_w, up_w, mine_ref, send_ref, *, width, chunk):
    half = mine_ref.shape[0]
    da, du = da_ref[...], du_ref[...]

    def turned(a, b):
        return lax.dot_general(a, b, CONTRACT_COLS, preferred_element_type=jnp.float32)

    for c in range(width // chunk):
        span = pl.ds(c * chunk, chunk)
        part = turned(da, gate_w[span, :]) + turned(du, up_w[span, :])
        part = part.astype(jnp.bfloat16)
        mine_ref[:, span] = part[:half]
        send_ref[:, span] = part[half:]
    last = pl.ds(width, LANES)
    mine_ref[:, last] = term_ref[:half, :]
    send_ref[:, last] = term_ref[half:, :]


def hidden_terms(held, other, weights, loads):
    count, columns = held.shape
    width, hid = weights[0].shape
    chunk = next(c for c in (1024, 512, 256, 128) if width % c == 0)
    me = lax.axis_index("node").astype(jnp.int32).reshape(1)
    unit = jax.ShapeDtypeStruct((2 * count, hid), jnp.bfloat16)
    shapes = (unit, unit, unit, jax.ShapeDtypeStruct((2 * count, LANES), jnp.bfloat16))
    if loads:
        shapes += tuple(pltpu.VMEM(w.shape, w.dtype) for w in weights)
    space = pl.ANY if loads else pltpu.VMEM
    place = in_hbm if loads else in_vmem
    *terms, = pl.pallas_call(
        functools.partial(hidden_kernel, width=width, chunk=chunk, loads=loads),
        out_shape=shapes,
        in_specs=[
            pl.BlockSpec(memory_space=pltpu.SMEM),
            *whole(2),
            *(pl.BlockSpec(memory_space=space),) * 3,
        ],
        out_specs=whole(len(shapes)),
        scratch_shapes=[pltpu.SemaphoreType.DMA((3, width // chunk))] if loads else [],
        compiler_params=pltpu.CompilerParams(vmem_limit_bytes=8 << 20),
        cost_estimate=NO_COST,
    )(me, held, other, *(place(w) for w in weights))
    return terms[:4], terms[4:] or weights


def row_terms(hidden, weights):
    da, du, _, term = hidden
    width = weights[0].shape[0]
    chunk = next(c for c in (1024, 512, 256, 128) if width % c == 0)
    back = jax.ShapeDtypeStruct((da.shape[0] // 2, width + LANES), jnp.bfloat16)
    return pl.pallas_call(
        functools.partial(rows_kernel, width=width, chunk=chunk),
        out_shape=(back, back),
        in_specs=list(whole(5)),
        out_specs=whole(2),
        compiler_params=pltpu.CompilerParams(vmem_limit_bytes=8 << 20),
        cost_estimate=NO_COST,
    )(da, du, term, *(in_vmem(w) for w in weights[:2]))


def dense(tokens, grad_out, expert_ids, gate_weights, w_gate, w_up, w_down):
    tok_count, width = tokens.shape
    node_count = lax.axis_size("node")
    local_count = lax.axis_size("local")
    clock = []

    def tick(*values):
        held = lax.optimization_barrier((*values, *clock))[: len(values)]
        return held[0] if len(values) == 1 else held

    def tock(value):
        clock[:] = [value]
        return value

    def permute(value, target):
        pairs = []
        for node in range(node_count):
            for place in range(local_count):
                to_node, to_place = target(node, place)
                pairs.append((node * local_count + place, to_node * local_count + to_place))
        return lax.ppermute(value, AXES, pairs)

    def cross(value, step):
        return permute(value, lambda n, p: (n ^ (2 if (n % 2 == 0) == (step == 0) else 4), p))

    def sibling(value):
        return permute(value, lambda n, p: (n ^ 1, p))

    def rotate(value, k):
        return permute(value, lambda n, p: (n, (p + k) % local_count))

    def along(value, bits):
        return permute(value, lambda n, p: (n, p ^ bits))

    def joined(*values):
        return jnp.concatenate(values, axis=1)

    own = pack(tokens, grad_out, expert_ids, gate_weights)[None, None]


    def terms(held, other, weights, loads):
        flat = [v.reshape(-1, v.shape[-1]) for v in (held, other)]
        return hidden_terms(*flat, weights, loads)

    def summed(mine, received):
        total = mine.astype(jnp.float32) + received.astype(jnp.float32)
        return total.reshape(-1, 4, tok_count, total.shape[-1]).astype(jnp.bfloat16)

    def folded(total, received):
        keep = received.shape[1]
        return (total[:, :keep].astype(jnp.float32) + received.astype(jnp.float32)).astype(jnp.bfloat16)

    def upper(total):
        return total[:, total.shape[1] // 2 :]


    weights = (w_gate[0], w_up[0], w_down[0])
    u_in = rotate(own, -1)
    v_in = rotate(own, 1)
    near_x = cross(own, 0)
    near_y = cross(own, 1)
    u = tock(tick(u_in))
    u_x = cross(u, 0)
    w_in = rotate(u, -1)
    near, near_x, near_y = tick(own, near_x, near_y)
    near = tock(joined(near, near_x, near_y))
    near_xy = cross(near_x, 1)
    v = tock(tick(v_in))
    v_x = cross(v, 0)
    u = tock(joined(*tick(u, u_x)))
    u_y = cross(u, 1)
    w = tock(tick(w_in))
    w_x = cross(w, 0)
    v = tock(joined(*tick(v, v_x)))
    v_y = cross(v, 1)
    near = tock(joined(*tick(near, near_xy)))
    u = joined(*tick(u, u_y))
    first = tock(jnp.concatenate((near, u), axis=0))
    first_other = sibling(first)
    w = tock(joined(*tick(w, w_x)))
    w_y = cross(w, 1)
    first_hidden, weights = terms(*tick(first, first_other), weights, True)
    tock(first_hidden[0])
    v = tock(joined(*tick(v, v_y)))
    w = joined(*tick(w, w_y))
    second = tock(jnp.concatenate((v, w), axis=0))
    second_other = sibling(second)
    first_mine, first_send = row_terms([tick(first_hidden[0]), *first_hidden[1:]], weights)
    tock(first_mine)
    first_back = sibling(first_send)
    second_hidden, _ = terms(*tick(second, second_other), weights, False)
    tock(second_hidden[0])
    first_sum = tock(summed(*tick(first_mine, first_back)))
    first_r1 = cross(upper(first_sum), 1)
    second_mine, second_send = row_terms([tick(second_hidden[0]), *second_hidden[1:]], weights)
    tock(second_mine)
    second_back = [sibling(v) for v in jnp.split(second_send, 1)]
    first_sum = tock(folded(*tick(first_sum, first_r1)))
    second_mine, *second_back = tick(second_mine, *second_back)
    second_sum = tock(summed(second_mine, jnp.concatenate(second_back, axis=0)))
    second_r1 = cross(upper(second_sum), 1)
    first_sum = tock(tick(first_sum))
    first_r2 = cross(upper(first_sum), 0)
    second_sum = tock(folded(*tick(second_sum, second_r1)))
    second_r2 = cross(upper(second_sum), 0)
    first_sum = tock(folded(*tick(first_sum, first_r2)))
    from_u = rotate(first_sum[1], 1)
    second_sum = tock(folded(*tick(second_sum, second_r2)))
    from_v = rotate(second_sum[0], -1)
    from_w = rotate(second_sum[1], 2)
    rows = [r.reshape(-1, r.shape[-1]) for r in (first, first_other, second, second_other)]
    rows[0] = tick(rows[0])
    sides = [[t[i] for t in (first_hidden, second_hidden)] for i in (0, 1, 2)]
    grad_gate_w, grad_up_w, grad_down = weight_terms(rows, *sides, width)
    tock(grad_down)
    from_u = tock(tick(from_u))
    ends = tick(first_sum[0], from_u, from_v, from_w)
    grad_in, grad_gate = finish([e[0] for e in ends], expert_ids)
    return (grad_in, grad_gate, grad_gate_w[None], grad_up_w[None], grad_down[None])


def slotted(tokens, grad_out, expert_ids, gate_weights, w_gate, w_up, w_down):
    tok_count = tokens.shape[0]
    width = tokens.shape[1]
    top_count = expert_ids.shape[1]
    node_count = lax.axis_size("node")
    local_count = lax.axis_size("local")
    capacity = max(2, 2 * tok_count * top_count // node_count)
    onehot = (
        expert_ids[:, :, None] == jnp.arange(node_count, dtype=jnp.int32)[None, None, :]
    ).astype(jnp.int32)
    per_token = jnp.sum(onehot, axis=1)
    earlier = jnp.cumsum(per_token, axis=0) - per_token
    slot_index = jnp.sum(earlier[:, None, :] * onehot, axis=2)
    flat_slot = expert_ids * capacity + slot_index
    placing = (
        flat_slot[:, :, None] == jnp.arange(node_count * capacity, dtype=jnp.int32)[None, None, :]
    ).astype(jnp.float32)
    placing_tok = jnp.sum(placing, axis=1).astype(jnp.bfloat16)
    send_in = (
        jnp.dot(placing_tok.T, tokens, preferred_element_type=jnp.float32)
        .astype(jnp.bfloat16)
        .reshape(node_count, capacity, width)
    )
    send_grad = (
        jnp.dot(placing_tok.T, grad_out, preferred_element_type=jnp.float32)
        .astype(jnp.bfloat16)
        .reshape(node_count, capacity, width)
    )
    send_gate = (
        jnp.einsum(
            "tks,tk->s", placing, gate_weights.astype(jnp.float32), precision=lax.Precision.HIGHEST
        )
        .astype(jnp.bfloat16)
        .reshape(node_count, capacity)
    )
    recv_in, recv_grad, recv_gate = (
        lax.all_to_all(send_in, "node", split_axis=0, concat_axis=0, tiled=True),
        lax.all_to_all(send_grad, "node", split_axis=0, concat_axis=0, tiled=True),
        lax.all_to_all(send_gate, "node", split_axis=0, concat_axis=0, tiled=True),
    )
    rows_in, rows_grad, rows_gate = (
        lax.all_gather(recv_in[None], "local", axis=0, tiled=True),
        lax.all_gather(recv_grad[None], "local", axis=0, tiled=True),
        lax.all_gather(recv_gate[None], "local", axis=0, tiled=True),
    )
    rows_total = local_count * node_count * capacity
    flat_in = rows_in.reshape(rows_total, width)
    flat_grad = rows_grad.reshape(rows_total, width)
    flat_gate = rows_gate.reshape(rows_total).astype(jnp.float32)
    gate_proj = w_gate[0]
    up_proj = w_up[0]
    down_proj = w_down[0]
    contract_rows = (((0,), (0,)), ((), ()))
    contract_cols = (((1,), (1,)), ((), ()))
    gate_pre = jnp.dot(flat_in, gate_proj, preferred_element_type=jnp.float32)
    up_pre = jnp.dot(flat_in, up_proj, preferred_element_type=jnp.float32)
    sigmoid_val = jax.nn.sigmoid(gate_pre)
    activated = gate_pre * sigmoid_val
    slope = sigmoid_val * (1.0 + gate_pre * (1.0 - sigmoid_val))
    hidden = (activated * up_pre).astype(jnp.bfloat16)
    grad_hidden = lax.dot_general(
        flat_grad, down_proj, contract_cols, preferred_element_type=jnp.float32
    )
    gate_partial = jnp.sum(hidden.astype(jnp.float32) * grad_hidden, axis=1)
    scaled = flat_gate[:, None] * grad_hidden
    grad_gate_pre = (scaled * up_pre * slope).astype(jnp.bfloat16)
    grad_up_pre = (scaled * activated).astype(jnp.bfloat16)
    weighted = (flat_gate[:, None] * hidden.astype(jnp.float32)).astype(jnp.bfloat16)
    grad_down = lax.dot_general(
        weighted, flat_grad, contract_rows, preferred_element_type=jnp.float32
    ).astype(jnp.bfloat16)
    grad_gate_w = lax.dot_general(
        flat_in, grad_gate_pre, contract_rows, preferred_element_type=jnp.float32
    ).astype(jnp.bfloat16)
    grad_up_w = lax.dot_general(
        flat_in, grad_up_pre, contract_rows, preferred_element_type=jnp.float32
    ).astype(jnp.bfloat16)
    input_partial = lax.dot_general(
        grad_gate_pre, gate_proj, contract_cols, preferred_element_type=jnp.float32
    )
    input_partial = input_partial + lax.dot_general(
        grad_up_pre, up_proj, contract_cols, preferred_element_type=jnp.float32
    )
    input_blocks = input_partial.reshape(local_count, node_count, capacity, width)
    gate_blocks = gate_partial.reshape(local_count, node_count, capacity)
    summed_in, summed_gate = (
        lax.psum_scatter(
            input_blocks.astype(jnp.bfloat16), "local", scatter_dimension=0, tiled=True
        ).astype(jnp.float32),
        lax.psum_scatter(
            gate_blocks.astype(jnp.bfloat16), "local", scatter_dimension=0, tiled=True
        ).astype(jnp.float32),
    )
    back_in, back_gate = (
        lax.all_to_all(
            summed_in[0].astype(jnp.bfloat16), "node", split_axis=0, concat_axis=0, tiled=True
        ),
        lax.all_to_all(
            summed_gate[0].astype(jnp.bfloat16), "node", split_axis=0, concat_axis=0, tiled=True
        ),
    )
    grad_in = jnp.dot(
        placing_tok,
        back_in.reshape(node_count * capacity, width),
        preferred_element_type=jnp.float32,
    ).astype(jnp.bfloat16)
    grad_gate = jnp.einsum(
        "tks,s->tk",
        placing,
        back_gate.reshape(node_count * capacity).astype(jnp.float32),
        precision=lax.Precision.HIGHEST,
    ).astype(jnp.bfloat16)
    return (grad_in, grad_gate, grad_gate_w[None], grad_up_w[None], grad_down[None])


def per_device(tokens, grad_out, expert_ids, gate_weights, w_gate, w_up, w_down):
    tok_count, top_count = expert_ids.shape
    node_count = lax.axis_size("node")
    capacity = max(2, 2 * tok_count * top_count // node_count)
    paired = node_count == 8 and lax.axis_size("local") == 4
    plan = dense if capacity >= tok_count and paired else slotted
    return plan(tokens, grad_out, expert_ids, gate_weights, w_gate, w_up, w_down)


def solution(mesh):
    placed = (
        P(("node", "local"), None),
        P(("node", "local"), None),
        P(("node", "local"), None),
        P(("node", "local"), None),
        P("node", None, "local"),
        P("node", None, "local"),
        P("node", "local", None),
    )
    return jax.shard_map(
        per_device,
        mesh=mesh,
        in_specs=placed,
        out_specs=(
            P(("node", "local"), None),
            P(("node", "local"), None),
            P("node", None, "local"),
            P("node", None, "local"),
            P("node", "local", None),
        ),
        check_vma=False,
    )
```

```python
import functools

import jax
import jax.numpy as jnp
from jax import lax
from jax.experimental import pallas as pl
from jax.experimental.pallas import tpu as pltpu
from jax.sharding import PartitionSpec as P

AXES = ("node", "local")
LANES = 128
SLOTS = 4
NO_COST = pl.CostEstimate(flops=0, bytes_accessed=0, transcendentals=0)
CONTRACT_ROWS = (((0,), (0,)), ((), ()))
CONTRACT_COLS = (((1,), (1,)), ((), ()))


def whole(count):
    return (pl.BlockSpec(memory_space=pltpu.VMEM),) * count


def in_hbm(value):
    return pltpu.with_memory_space_constraint(value, pltpu.HBM)


def load_kernel(*refs):
    *refs, sems = refs
    count = len(refs) // 2
    copies = [pltpu.make_async_copy(refs[i], refs[count + i], sems.at[i]) for i in range(count)]
    for copy in copies:
        copy.start()
    for copy in copies:
        copy.wait()


def load(*values):
    return pl.pallas_call(
        load_kernel,
        out_shape=tuple(pltpu.VMEM(v.shape, v.dtype) for v in values),
        in_specs=[pl.BlockSpec(memory_space=pl.ANY)] * len(values),
        out_specs=whole(len(values)),
        scratch_shapes=[pltpu.SemaphoreType.DMA((len(values),))],
        compiler_params=pltpu.CompilerParams(vmem_limit_bytes=1 << 20),
        cost_estimate=NO_COST,
    )(*(in_hbm(v) for v in values))


def pack_kernel(
    tokens_hbm, grad_hbm, ids_hbm, gates_hbm, own_ref, ids_ref, gates_ref, square, sems
):
    width = tokens_hbm.shape[1]
    pairs = (
        (ids_hbm, ids_ref),
        (gates_hbm, gates_ref),
        (tokens_hbm, own_ref.at[:, pl.ds(0, width)]),
        (grad_hbm, own_ref.at[:, pl.ds(width, width)]),
    )
    copies = [pltpu.make_async_copy(*pair, sems.at[i]) for i, pair in enumerate(pairs)]
    for copy in copies:
        copy.start()
    copies[0].wait()
    copies[1].wait()
    ids, gates = ids_ref[...], gates_ref[...].astype(jnp.float32)
    top_count, tok_count = ids.shape
    experts = lax.broadcasted_iota(jnp.int32, (LANES, tok_count), 0)
    table = jnp.zeros(experts.shape, jnp.float32)
    for k in range(top_count):
        table = table + jnp.where(experts == ids[k : k + 1], gates[k : k + 1], 0.0)
    square[...] = jnp.zeros(square.shape, jnp.float32)
    square[:, :tok_count] = table
    own_ref[:, 2 * width :] = square[...].T[:tok_count].astype(jnp.bfloat16)
    copies[2].wait()
    copies[3].wait()


def pack(tokens, grad_out, expert_ids, gate_weights):
    rows, width = tokens.shape
    hbm = pl.BlockSpec(memory_space=pl.ANY)
    return pl.pallas_call(
        pack_kernel,
        out_shape=jax.ShapeDtypeStruct((rows, 2 * width + LANES), tokens.dtype),
        in_specs=[hbm] * 4,
        out_specs=whole(1)[0],
        scratch_shapes=[
            pltpu.VMEM(expert_ids.T.shape, expert_ids.dtype),
            pltpu.VMEM(gate_weights.T.shape, gate_weights.dtype),
            pltpu.VMEM((LANES, LANES), jnp.float32),
            pltpu.SemaphoreType.DMA((4,)),
        ],
        compiler_params=pltpu.CompilerParams(vmem_limit_bytes=2 << 20),
        cost_estimate=NO_COST,
    )(*(in_hbm(v) for v in (tokens, grad_out, expert_ids.T, gate_weights.T)))


def finish_kernel(*refs):
    *terms, ids_ref, rows_ref, gates_ref, square = refs
    width = rows_ref.shape[1]
    total = terms[0][...].astype(jnp.float32)
    for term in terms[1:]:
        total = total + term[...].astype(jnp.float32)
    rows_ref[...] = total[:, :width].astype(jnp.bfloat16)
    ids = ids_ref[...]
    top_count, tok_count = ids.shape
    square[...] = jnp.zeros(square.shape, jnp.float32)
    square[:tok_count] = total[:, width:].astype(jnp.bfloat16).astype(jnp.float32)
    sums = square[...].T[:, :tok_count]
    experts = lax.broadcasted_iota(jnp.int32, sums.shape, 0)
    slots = lax.broadcasted_iota(jnp.int32, ids.shape, 0)
    picked = jnp.zeros(ids.shape, jnp.float32)
    for k in range(top_count):
        value = jnp.sum(jnp.where(experts == ids[k : k + 1], sums, 0.0), axis=0, keepdims=True)
        picked = picked + jnp.where(slots == k, value, 0.0)
    gates_ref[...] = picked.astype(jnp.bfloat16)


def finish(terms, expert_ids):
    rows, columns = terms[0].shape
    ids = expert_ids.T
    grad_in, grad_gate = pl.pallas_call(
        finish_kernel,
        out_shape=(
            jax.ShapeDtypeStruct((rows, columns - LANES), jnp.bfloat16),
            jax.ShapeDtypeStruct(ids.shape, jnp.bfloat16),
        ),
        in_specs=list(whole(len(terms) + 1)),
        out_specs=whole(2),
        scratch_shapes=[pltpu.VMEM((LANES, LANES), jnp.float32)],
        compiler_params=pltpu.CompilerParams(vmem_limit_bytes=2 << 20),
        cost_estimate=NO_COST,
    )(*terms, ids)
    return grad_in, grad_gate.T


def weights_kernel(*refs, blocks, groups, width, chunk):
    rows, refs = refs[:blocks], refs[blocks:]
    da, du, hw, refs = refs[:groups], refs[groups : 2 * groups], refs[2 * groups : 3 * groups], refs[3 * groups :]
    outs, parts, sems = refs[:3], refs[3:6], refs[6]

    def stacked(pieces, span=slice(None)):
        return jnp.concatenate([p[:, span] for p in pieces], axis=0)

    def outer(left, right):
        product = lax.dot_general(left, right, CONTRACT_ROWS, preferred_element_type=jnp.float32)
        return product.astype(jnp.bfloat16)

    gate_side, up_side, down_side = stacked(da), stacked(du), stacked(hw)
    copies = []
    for c in range(width // chunk):
        slot, span = c % SLOTS, pl.ds(c * chunk, chunk)
        for copy in copies[c - SLOTS] if c >= SLOTS else ():
            copy.wait()
        part_in = stacked(rows, span)
        parts[0][slot] = outer(part_in, gate_side)
        parts[1][slot] = outer(part_in, up_side)
        parts[2][slot] = outer(down_side, stacked(rows, pl.ds(width + c * chunk, chunk)))
        places = ((span, slice(None)), (span, slice(None)), (slice(None), span))
        copies.append(
            [
                pltpu.make_async_copy(parts[i].at[slot], outs[i].at[place], sems.at[i, slot])
                for i, place in enumerate(places)
            ]
        )
        for copy in copies[-1]:
            copy.start()
    for copy in sum(copies[-SLOTS:], []):
        copy.wait()


def weight_terms(rows, da, du, hw, width):
    hid = da[0].shape[1]
    chunk = next(c for c in (1024, 512, 256, 128) if width % c == 0)
    shapes = ((width, hid), (width, hid), (hid, width))
    hbm = pl.BlockSpec(memory_space=pl.ANY)
    return pl.pallas_call(
        functools.partial(
            weights_kernel, blocks=len(rows), groups=len(da), width=width, chunk=chunk
        ),
        out_shape=tuple(jax.ShapeDtypeStruct(s, jnp.bfloat16) for s in shapes),
        in_specs=list(whole(len(rows) + 3 * len(da))),
        out_specs=(hbm,) * 3,
        scratch_shapes=[
            pltpu.VMEM((SLOTS, chunk, hid), jnp.bfloat16),
            pltpu.VMEM((SLOTS, chunk, hid), jnp.bfloat16),
            pltpu.VMEM((SLOTS, hid, chunk), jnp.bfloat16),
            pltpu.SemaphoreType.DMA((3, SLOTS)),
        ],
        compiler_params=pltpu.CompilerParams(vmem_limit_bytes=16 << 20),
        cost_estimate=pl.CostEstimate(
            flops=0, bytes_accessed=16 << 18, transcendentals=0
        ),
    )(*rows, *da, *du, *hw)


def in_vmem(value):
    return pltpu.with_memory_space_constraint(value, pltpu.VMEM)


def hidden_kernel(*refs, width, chunk, loads):
    me_ref, held_ref, other_ref = refs[:3]
    sources, refs = refs[3:6], refs[6:]
    da_ref, du_ref, hw_ref, term_ref = refs[:4]
    spans = [pl.ds(c * chunk, chunk) for c in range(width // chunk)]
    copies = [[] for _ in spans]
    gate_w, up_w, down_w = refs[4:7] if loads else sources
    if loads:
        sems = refs[7]
        for c, span in enumerate(spans):
            places = ((span, slice(None)), (span, slice(None)), (slice(None), span))
            for i, place in enumerate(places):
                copies[c].append(
                    pltpu.make_async_copy(sources[i].at[place], refs[4 + i].at[place], sems.at[i, c])
                )
                copies[c][-1].start()

    def rows(start, size):
        span = pl.ds(start, size)
        return jnp.concatenate([held_ref[:, span], other_ref[:, span]], axis=0)

    extra = rows(2 * width, LANES).astype(jnp.float32)
    named = lax.broadcasted_iota(jnp.int32, extra.shape, 1) == me_ref[0]
    flat_gate = jnp.sum(jnp.where(named, extra, 0.0), axis=1, keepdims=True)

    def plain(a, b):
        return lax.dot_general(a, b, (((1,), (0,)), ((), ())), preferred_element_type=jnp.float32)

    def turned(a, b):
        return lax.dot_general(a, b, CONTRACT_COLS, preferred_element_type=jnp.float32)

    gate_pre = up_pre = grad_hidden = 0.0
    for c, span in enumerate(spans):
        for copy in copies[c]:
            copy.wait()
        part_in = rows(c * chunk, chunk)
        gate_pre += plain(part_in, gate_w[span, :])
        up_pre += plain(part_in, up_w[span, :])
        grad_hidden += turned(rows(width + c * chunk, chunk), down_w[:, span])
    sigmoid_val = jax.nn.sigmoid(gate_pre)
    activated = gate_pre * sigmoid_val
    slope = sigmoid_val * (1.0 + gate_pre * (1.0 - sigmoid_val))
    hidden = (activated * up_pre).astype(jnp.bfloat16).astype(jnp.float32)
    gate_partial = jnp.sum(hidden * grad_hidden, axis=1, keepdims=True)
    scaled = flat_gate * grad_hidden
    grad_gate_pre = (scaled * up_pre * slope).astype(jnp.bfloat16)
    grad_up_pre = (scaled * activated).astype(jnp.bfloat16)
    da_ref[...] = grad_gate_pre
    du_ref[...] = grad_up_pre
    hw_ref[...] = (flat_gate * hidden).astype(jnp.bfloat16)
    term_ref[...] = jnp.where(named, gate_partial, 0.0).astype(jnp.bfloat16)


def rows_kernel(da_ref, du_ref, term_ref, gate_w, up_w, mine_ref, send_ref, *, width, chunk):
    half = mine_ref.shape[0]
    da, du = da_ref[...], du_ref[...]

    def turned(a, b):
        return lax.dot_general(a, b, CONTRACT_COLS, preferred_element_type=jnp.float32)

    for c in range(width // chunk):
        span = pl.ds(c * chunk, chunk)
        part = turned(da, gate_w[span, :]) + turned(du, up_w[span, :])
        part = part.astype(jnp.bfloat16)
        mine_ref[:, span] = part[:half]
        send_ref[:, span] = part[half:]
    last = pl.ds(width, LANES)
    mine_ref[:, last] = term_ref[:half, :]
    send_ref[:, last] = term_ref[half:, :]


def hidden_terms(held, other, weights, loads):
    count, columns = held.shape
    width, hid = weights[0].shape
    chunk = next(c for c in (1024, 512, 256, 128) if width % c == 0)
    me = lax.axis_index("node").astype(jnp.int32).reshape(1)
    unit = jax.ShapeDtypeStruct((2 * count, hid), jnp.bfloat16)
    shapes = (unit, unit, unit, jax.ShapeDtypeStruct((2 * count, LANES), jnp.bfloat16))
    if loads:
        shapes += tuple(pltpu.VMEM(w.shape, w.dtype) for w in weights)
    space = pl.ANY if loads else pltpu.VMEM
    place = in_hbm if loads else in_vmem
    *terms, = pl.pallas_call(
        functools.partial(hidden_kernel, width=width, chunk=chunk, loads=loads),
        out_shape=shapes,
        in_specs=[
            pl.BlockSpec(memory_space=pltpu.SMEM),
            *whole(2),
            *(pl.BlockSpec(memory_space=space),) * 3,
        ],
        out_specs=whole(len(shapes)),
        scratch_shapes=[pltpu.SemaphoreType.DMA((3, width // chunk))] if loads else [],
        compiler_params=pltpu.CompilerParams(vmem_limit_bytes=8 << 20),
        cost_estimate=NO_COST,
    )(me, held, other, *(place(w) for w in weights))
    return terms[:4], terms[4:] or weights


def row_terms(hidden, weights):
    da, du, _, term = hidden
    width = weights[0].shape[0]
    chunk = next(c for c in (1024, 512, 256, 128) if width % c == 0)
    back = jax.ShapeDtypeStruct((da.shape[0] // 2, width + LANES), jnp.bfloat16)
    return pl.pallas_call(
        functools.partial(rows_kernel, width=width, chunk=chunk),
        out_shape=(back, back),
        in_specs=list(whole(5)),
        out_specs=whole(2),
        compiler_params=pltpu.CompilerParams(vmem_limit_bytes=8 << 20),
        cost_estimate=NO_COST,
    )(da, du, term, *(in_vmem(w) for w in weights[:2]))


def dense(tokens, grad_out, expert_ids, gate_weights, w_gate, w_up, w_down):
    tok_count, width = tokens.shape
    node_count = lax.axis_size("node")
    local_count = lax.axis_size("local")
    clock = []

    def tick(*values):
        held = lax.optimization_barrier((*values, *clock))[: len(values)]
        return held[0] if len(values) == 1 else held

    def tock(value):
        clock[:] = [value]
        return value

    def permute(value, target):
        pairs = []
        for node in range(node_count):
            for place in range(local_count):
                to_node, to_place = target(node, place)
                pairs.append((node * local_count + place, to_node * local_count + to_place))
        return lax.ppermute(value, AXES, pairs)

    def cross(value, step):
        return permute(value, lambda n, p: (n ^ (2 if (n % 2 == 0) == (step == 0) else 4), p))

    def sibling(value):
        return permute(value, lambda n, p: (n ^ 1, p))

    def rotate(value, k):
        return permute(value, lambda n, p: (n, (p + k) % local_count))

    def along(value, bits):
        return permute(value, lambda n, p: (n, p ^ bits))

    def joined(*values):
        return jnp.concatenate(values, axis=1)

    own = pack(tokens, grad_out, expert_ids, gate_weights)[None, None]


    def terms(held, other, weights, loads):
        flat = [v.reshape(-1, v.shape[-1]) for v in (held, other)]
        return hidden_terms(*flat, weights, loads)

    def summed(mine, received):
        total = mine.astype(jnp.float32) + received.astype(jnp.float32)
        return total.reshape(-1, 4, tok_count, total.shape[-1]).astype(jnp.bfloat16)

    def folded(total, received):
        keep = received.shape[1]
        return (total[:, :keep].astype(jnp.float32) + received.astype(jnp.float32)).astype(jnp.bfloat16)

    def upper(total):
        return total[:, total.shape[1] // 2 :]


    weights = (w_gate[0], w_up[0], w_down[0])
    u_in = rotate(own, -1)
    v_in = rotate(own, 1)
    near_x = cross(own, 0)
    near_y = cross(own, 1)
    u = tock(tick(u_in))
    u_x = cross(u, 0)
    w_in = rotate(u, -1)
    near, near_x, near_y = tick(own, near_x, near_y)
    near = tock(joined(near, near_x, near_y))
    near_xy = cross(near_x, 1)
    v = tock(tick(v_in))
    v_x = cross(v, 0)
    u = tock(joined(*tick(u, u_x)))
    u_y = cross(u, 1)
    w = tock(tick(w_in))
    w_x = cross(w, 0)
    weights = load(*tick(*weights, own)[:3])
    tock(weights[0])
    v = tock(joined(*tick(v, v_x)))
    v_y = cross(v, 1)
    near = tock(joined(*tick(near, near_xy)))
    u = joined(*tick(u, u_y))
    first = tock(jnp.concatenate((near, u), axis=0))
    first_other = sibling(first)
    w = tock(joined(*tick(w, w_x)))
    w_y = cross(w, 1)
    first_hidden, weights = terms(*tick(first, first_other), weights, False)
    tock(first_hidden[0])
    first_mine, first_send = row_terms([tick(first_hidden[0]), *first_hidden[1:]], weights)
    tock(first_mine)
    first_back = sibling(first_send)
    v = tock(joined(*tick(v, v_y)))
    w = joined(*tick(w, w_y))
    second = tock(jnp.concatenate((v, w), axis=0))
    second_other = sibling(second)
    first_sum = tock(summed(*tick(first_mine, first_back)))
    first_r1 = cross(upper(first_sum), 1)
    second_hidden, _ = terms(*tick(second, second_other), weights, False)
    tock(second_hidden[0])
    second_mine, second_send = row_terms([tick(second_hidden[0]), *second_hidden[1:]], weights)
    tock(second_mine)
    second_back = [sibling(v) for v in jnp.split(second_send, 1)]
    first_sum = tock(folded(*tick(first_sum, first_r1)))
    first_sum = tock(tick(first_sum))
    first_r2 = cross(upper(first_sum), 0)
    second_mine, *second_back = tick(second_mine, *second_back)
    second_sum = tock(summed(second_mine, jnp.concatenate(second_back, axis=0)))
    cut = width // 2
    lo, hi = second_sum[..., :cut], second_sum[..., cut:]
    lo_r1 = cross(upper(lo), 1)
    hi_r1 = cross(upper(hi), 1)
    lo = tock(folded(*tick(lo, lo_r1)))
    lo_r2 = cross(upper(lo), 0)
    hi = tock(folded(*tick(hi, hi_r1)))
    hi_r2 = cross(upper(hi), 0)
    first_sum = tock(folded(*tick(first_sum, first_r2)))
    from_u = rotate(first_sum[1], 1)
    lo, lo_r2, hi, hi_r2 = tick(lo, lo_r2, hi, hi_r2)
    second_sum = tock(jnp.concatenate((folded(lo, lo_r2), folded(hi, hi_r2)), axis=-1))
    from_v = rotate(second_sum[0], -1)
    from_w = rotate(second_sum[1], 2)
    rows = [r.reshape(-1, r.shape[-1]) for r in (first, first_other, second, second_other)]
    rows[0] = tick(rows[0])
    sides = [[t[i] for t in (first_hidden, second_hidden)] for i in (0, 1, 2)]
    grad_gate_w, grad_up_w, grad_down = weight_terms(rows, *sides, width)
    tock(grad_down)
    from_u = tock(tick(from_u))
    ends = tick(first_sum[0], from_u, from_v, from_w)
    grad_in, grad_gate = finish([e[0] for e in ends], expert_ids)
    return (grad_in, grad_gate, grad_gate_w[None], grad_up_w[None], grad_down[None])


def slotted(tokens, grad_out, expert_ids, gate_weights, w_gate, w_up, w_down):
    tok_count = tokens.shape[0]
    width = tokens.shape[1]
    top_count = expert_ids.shape[1]
    node_count = lax.axis_size("node")
    local_count = lax.axis_size("local")
    capacity = max(2, 2 * tok_count * top_count // node_count)
    onehot = (
        expert_ids[:, :, None] == jnp.arange(node_count, dtype=jnp.int32)[None, None, :]
    ).astype(jnp.int32)
    per_token = jnp.sum(onehot, axis=1)
    earlier = jnp.cumsum(per_token, axis=0) - per_token
    slot_index = jnp.sum(earlier[:, None, :] * onehot, axis=2)
    flat_slot = expert_ids * capacity + slot_index
    placing = (
        flat_slot[:, :, None] == jnp.arange(node_count * capacity, dtype=jnp.int32)[None, None, :]
    ).astype(jnp.float32)
    placing_tok = jnp.sum(placing, axis=1).astype(jnp.bfloat16)
    send_in = (
        jnp.dot(placing_tok.T, tokens, preferred_element_type=jnp.float32)
        .astype(jnp.bfloat16)
        .reshape(node_count, capacity, width)
    )
    send_grad = (
        jnp.dot(placing_tok.T, grad_out, preferred_element_type=jnp.float32)
        .astype(jnp.bfloat16)
        .reshape(node_count, capacity, width)
    )
    send_gate = (
        jnp.einsum(
            "tks,tk->s", placing, gate_weights.astype(jnp.float32), precision=lax.Precision.HIGHEST
        )
        .astype(jnp.bfloat16)
        .reshape(node_count, capacity)
    )
    recv_in, recv_grad, recv_gate = (
        lax.all_to_all(send_in, "node", split_axis=0, concat_axis=0, tiled=True),
        lax.all_to_all(send_grad, "node", split_axis=0, concat_axis=0, tiled=True),
        lax.all_to_all(send_gate, "node", split_axis=0, concat_axis=0, tiled=True),
    )
    rows_in, rows_grad, rows_gate = (
        lax.all_gather(recv_in[None], "local", axis=0, tiled=True),
        lax.all_gather(recv_grad[None], "local", axis=0, tiled=True),
        lax.all_gather(recv_gate[None], "local", axis=0, tiled=True),
    )
    rows_total = local_count * node_count * capacity
    flat_in = rows_in.reshape(rows_total, width)
    flat_grad = rows_grad.reshape(rows_total, width)
    flat_gate = rows_gate.reshape(rows_total).astype(jnp.float32)
    gate_proj = w_gate[0]
    up_proj = w_up[0]
    down_proj = w_down[0]
    contract_rows = (((0,), (0,)), ((), ()))
    contract_cols = (((1,), (1,)), ((), ()))
    gate_pre = jnp.dot(flat_in, gate_proj, preferred_element_type=jnp.float32)
    up_pre = jnp.dot(flat_in, up_proj, preferred_element_type=jnp.float32)
    sigmoid_val = jax.nn.sigmoid(gate_pre)
    activated = gate_pre * sigmoid_val
    slope = sigmoid_val * (1.0 + gate_pre * (1.0 - sigmoid_val))
    hidden = (activated * up_pre).astype(jnp.bfloat16)
    grad_hidden = lax.dot_general(
        flat_grad, down_proj, contract_cols, preferred_element_type=jnp.float32
    )
    gate_partial = jnp.sum(hidden.astype(jnp.float32) * grad_hidden, axis=1)
    scaled = flat_gate[:, None] * grad_hidden
    grad_gate_pre = (scaled * up_pre * slope).astype(jnp.bfloat16)
    grad_up_pre = (scaled * activated).astype(jnp.bfloat16)
    weighted = (flat_gate[:, None] * hidden.astype(jnp.float32)).astype(jnp.bfloat16)
    grad_down = lax.dot_general(
        weighted, flat_grad, contract_rows, preferred_element_type=jnp.float32
    ).astype(jnp.bfloat16)
    grad_gate_w = lax.dot_general(
        flat_in, grad_gate_pre, contract_rows, preferred_element_type=jnp.float32
    ).astype(jnp.bfloat16)
    grad_up_w = lax.dot_general(
        flat_in, grad_up_pre, contract_rows, preferred_element_type=jnp.float32
    ).astype(jnp.bfloat16)
    input_partial = lax.dot_general(
        grad_gate_pre, gate_proj, contract_cols, preferred_element_type=jnp.float32
    )
    input_partial = input_partial + lax.dot_general(
        grad_up_pre, up_proj, contract_cols, preferred_element_type=jnp.float32
    )
    input_blocks = input_partial.reshape(local_count, node_count, capacity, width)
    gate_blocks = gate_partial.reshape(local_count, node_count, capacity)
    summed_in, summed_gate = (
        lax.psum_scatter(
            input_blocks.astype(jnp.bfloat16), "local", scatter_dimension=0, tiled=True
        ).astype(jnp.float32),
        lax.psum_scatter(
            gate_blocks.astype(jnp.bfloat16), "local", scatter_dimension=0, tiled=True
        ).astype(jnp.float32),
    )
    back_in, back_gate = (
        lax.all_to_all(
            summed_in[0].astype(jnp.bfloat16), "node", split_axis=0, concat_axis=0, tiled=True
        ),
        lax.all_to_all(
            summed_gate[0].astype(jnp.bfloat16), "node", split_axis=0, concat_axis=0, tiled=True
        ),
    )
    grad_in = jnp.dot(
        placing_tok,
        back_in.reshape(node_count * capacity, width),
        preferred_element_type=jnp.float32,
    ).astype(jnp.bfloat16)
    grad_gate = jnp.einsum(
        "tks,s->tk",
        placing,
        back_gate.reshape(node_count * capacity).astype(jnp.float32),
        precision=lax.Precision.HIGHEST,
    ).astype(jnp.bfloat16)
    return (grad_in, grad_gate, grad_gate_w[None], grad_up_w[None], grad_down[None])


def per_device(tokens, grad_out, expert_ids, gate_weights, w_gate, w_up, w_down):
    tok_count, top_count = expert_ids.shape
    node_count = lax.axis_size("node")
    capacity = max(2, 2 * tok_count * top_count // node_count)
    paired = node_count == 8 and lax.axis_size("local") == 4
    plan = dense if capacity >= tok_count and paired else slotted
    return plan(tokens, grad_out, expert_ids, gate_weights, w_gate, w_up, w_down)


def solution(mesh):
    placed = (
        P(("node", "local"), None),
        P(("node", "local"), None),
        P(("node", "local"), None),
        P(("node", "local"), None),
        P("node", None, "local"),
        P("node", None, "local"),
        P("node", "local", None),
    )
    return jax.shard_map(
        per_device,
        mesh=mesh,
        in_specs=placed,
        out_specs=(
            P(("node", "local"), None),
            P(("node", "local"), None),
            P("node", None, "local"),
            P("node", None, "local"),
            P("node", "local", None),
        ),
        check_vma=False,
    )
```

```python
import functools

import jax
import jax.numpy as jnp
from jax import lax
from jax.experimental import pallas as pl
from jax.experimental.pallas import tpu as pltpu
from jax.sharding import PartitionSpec as P

AXES = ("node", "local")
LANES = 128
SLOTS = 4
NO_COST = pl.CostEstimate(flops=0, bytes_accessed=0, transcendentals=0)
CONTRACT_ROWS = (((0,), (0,)), ((), ()))
CONTRACT_COLS = (((1,), (1,)), ((), ()))


def whole(count):
    return (pl.BlockSpec(memory_space=pltpu.VMEM),) * count


def in_hbm(value):
    return pltpu.with_memory_space_constraint(value, pltpu.HBM)


def load_kernel(*refs):
    *refs, sems = refs
    count = len(refs) // 2
    copies = [pltpu.make_async_copy(refs[i], refs[count + i], sems.at[i]) for i in range(count)]
    for copy in copies:
        copy.start()
    for copy in copies:
        copy.wait()


def load(*values):
    return pl.pallas_call(
        load_kernel,
        out_shape=tuple(pltpu.VMEM(v.shape, v.dtype) for v in values),
        in_specs=[pl.BlockSpec(memory_space=pl.ANY)] * len(values),
        out_specs=whole(len(values)),
        scratch_shapes=[pltpu.SemaphoreType.DMA((len(values),))],
        compiler_params=pltpu.CompilerParams(vmem_limit_bytes=1 << 20),
        cost_estimate=NO_COST,
    )(*(in_hbm(v) for v in values))


def pack_kernel(
    tokens_hbm, grad_hbm, ids_hbm, gates_hbm, own_ref, ids_ref, gates_ref, square, sems
):
    width = tokens_hbm.shape[1]
    pairs = (
        (ids_hbm, ids_ref),
        (gates_hbm, gates_ref),
        (tokens_hbm, own_ref.at[:, pl.ds(0, width)]),
        (grad_hbm, own_ref.at[:, pl.ds(width, width)]),
    )
    copies = [pltpu.make_async_copy(*pair, sems.at[i]) for i, pair in enumerate(pairs)]
    for copy in copies:
        copy.start()
    copies[0].wait()
    copies[1].wait()
    ids, gates = ids_ref[...], gates_ref[...].astype(jnp.float32)
    top_count, tok_count = ids.shape
    experts = lax.broadcasted_iota(jnp.int32, (LANES, tok_count), 0)
    table = jnp.zeros(experts.shape, jnp.float32)
    for k in range(top_count):
        table = table + jnp.where(experts == ids[k : k + 1], gates[k : k + 1], 0.0)
    square[...] = jnp.zeros(square.shape, jnp.float32)
    square[:, :tok_count] = table
    own_ref[:, 2 * width :] = square[...].T[:tok_count].astype(jnp.bfloat16)
    copies[2].wait()
    copies[3].wait()


def pack(tokens, grad_out, expert_ids, gate_weights):
    rows, width = tokens.shape
    hbm = pl.BlockSpec(memory_space=pl.ANY)
    return pl.pallas_call(
        pack_kernel,
        out_shape=jax.ShapeDtypeStruct((rows, 2 * width + LANES), tokens.dtype),
        in_specs=[hbm] * 4,
        out_specs=whole(1)[0],
        scratch_shapes=[
            pltpu.VMEM(expert_ids.T.shape, expert_ids.dtype),
            pltpu.VMEM(gate_weights.T.shape, gate_weights.dtype),
            pltpu.VMEM((LANES, LANES), jnp.float32),
            pltpu.SemaphoreType.DMA((4,)),
        ],
        compiler_params=pltpu.CompilerParams(vmem_limit_bytes=2 << 20),
        cost_estimate=NO_COST,
    )(*(in_hbm(v) for v in (tokens, grad_out, expert_ids.T, gate_weights.T)))


def finish_kernel(*refs):
    *terms, ids_ref, rows_ref, gates_ref, square = refs
    width = rows_ref.shape[1]
    total = terms[0][...].astype(jnp.float32)
    for term in terms[1:]:
        total = total + term[...].astype(jnp.float32)
    rows_ref[...] = total[:, :width].astype(jnp.bfloat16)
    ids = ids_ref[...]
    top_count, tok_count = ids.shape
    square[...] = jnp.zeros(square.shape, jnp.float32)
    square[:tok_count] = total[:, width:].astype(jnp.bfloat16).astype(jnp.float32)
    sums = square[...].T[:, :tok_count]
    experts = lax.broadcasted_iota(jnp.int32, sums.shape, 0)
    slots = lax.broadcasted_iota(jnp.int32, ids.shape, 0)
    picked = jnp.zeros(ids.shape, jnp.float32)
    for k in range(top_count):
        value = jnp.sum(jnp.where(experts == ids[k : k + 1], sums, 0.0), axis=0, keepdims=True)
        picked = picked + jnp.where(slots == k, value, 0.0)
    gates_ref[...] = picked.astype(jnp.bfloat16)


def finish(terms, expert_ids):
    rows, columns = terms[0].shape
    ids = expert_ids.T
    grad_in, grad_gate = pl.pallas_call(
        finish_kernel,
        out_shape=(
            jax.ShapeDtypeStruct((rows, columns - LANES), jnp.bfloat16),
            jax.ShapeDtypeStruct(ids.shape, jnp.bfloat16),
        ),
        in_specs=list(whole(len(terms) + 1)),
        out_specs=whole(2),
        scratch_shapes=[pltpu.VMEM((LANES, LANES), jnp.float32)],
        compiler_params=pltpu.CompilerParams(vmem_limit_bytes=2 << 20),
        cost_estimate=NO_COST,
    )(*terms, ids)
    return grad_in, grad_gate.T


def weights_kernel(*refs, blocks, groups, width, chunk):
    rows, refs = refs[:blocks], refs[blocks:]
    da, du, hw, refs = refs[:groups], refs[groups : 2 * groups], refs[2 * groups : 3 * groups], refs[3 * groups :]
    outs, parts, sems = refs[:3], refs[3:6], refs[6]

    def stacked(pieces, span=slice(None)):
        return jnp.concatenate([p[:, span] for p in pieces], axis=0)

    def outer(left, right):
        product = lax.dot_general(left, right, CONTRACT_ROWS, preferred_element_type=jnp.float32)
        return product.astype(jnp.bfloat16)

    gate_side, up_side, down_side = stacked(da), stacked(du), stacked(hw)
    copies = []
    for c in range(width // chunk):
        slot, span = c % SLOTS, pl.ds(c * chunk, chunk)
        for copy in copies[c - SLOTS] if c >= SLOTS else ():
            copy.wait()
        part_in = stacked(rows, span)
        parts[0][slot] = outer(part_in, gate_side)
        parts[1][slot] = outer(part_in, up_side)
        parts[2][slot] = outer(down_side, stacked(rows, pl.ds(width + c * chunk, chunk)))
        places = ((span, slice(None)), (span, slice(None)), (slice(None), span))
        copies.append(
            [
                pltpu.make_async_copy(parts[i].at[slot], outs[i].at[place], sems.at[i, slot])
                for i, place in enumerate(places)
            ]
        )
        for copy in copies[-1]:
            copy.start()
    for copy in sum(copies[-SLOTS:], []):
        copy.wait()


def weight_terms(rows, da, du, hw, width):
    hid = da[0].shape[1]
    chunk = next(c for c in (1024, 512, 256, 128) if width % c == 0)
    shapes = ((width, hid), (width, hid), (hid, width))
    hbm = pl.BlockSpec(memory_space=pl.ANY)
    return pl.pallas_call(
        functools.partial(
            weights_kernel, blocks=len(rows), groups=len(da), width=width, chunk=chunk
        ),
        out_shape=tuple(jax.ShapeDtypeStruct(s, jnp.bfloat16) for s in shapes),
        in_specs=list(whole(len(rows) + 3 * len(da))),
        out_specs=(hbm,) * 3,
        scratch_shapes=[
            pltpu.VMEM((SLOTS, chunk, hid), jnp.bfloat16),
            pltpu.VMEM((SLOTS, chunk, hid), jnp.bfloat16),
            pltpu.VMEM((SLOTS, hid, chunk), jnp.bfloat16),
            pltpu.SemaphoreType.DMA((3, SLOTS)),
        ],
        compiler_params=pltpu.CompilerParams(vmem_limit_bytes=16 << 20),
        cost_estimate=pl.CostEstimate(
            flops=0, bytes_accessed=16 << 18, transcendentals=0
        ),
    )(*rows, *da, *du, *hw)


def in_vmem(value):
    return pltpu.with_memory_space_constraint(value, pltpu.VMEM)


def hidden_kernel(*refs, width, chunk, loads):
    me_ref, held_ref, other_ref = refs[:3]
    sources, refs = refs[3:6], refs[6:]
    da_ref, du_ref, hw_ref, term_ref = refs[:4]
    spans = [pl.ds(c * chunk, chunk) for c in range(width // chunk)]
    copies = [[] for _ in spans]
    gate_w, up_w, down_w = refs[4:7] if loads else sources
    if loads:
        sems = refs[7]
        for c, span in enumerate(spans):
            places = ((span, slice(None)), (span, slice(None)), (slice(None), span))
            for i, place in enumerate(places):
                copies[c].append(
                    pltpu.make_async_copy(sources[i].at[place], refs[4 + i].at[place], sems.at[i, c])
                )
                copies[c][-1].start()

    def rows(start, size):
        span = pl.ds(start, size)
        return jnp.concatenate([held_ref[:, span], other_ref[:, span]], axis=0)

    extra = rows(2 * width, LANES).astype(jnp.float32)
    named = lax.broadcasted_iota(jnp.int32, extra.shape, 1) == me_ref[0]
    flat_gate = jnp.sum(jnp.where(named, extra, 0.0), axis=1, keepdims=True)

    def plain(a, b):
        return lax.dot_general(a, b, (((1,), (0,)), ((), ())), preferred_element_type=jnp.float32)

    def turned(a, b):
        return lax.dot_general(a, b, CONTRACT_COLS, preferred_element_type=jnp.float32)

    gate_pre = up_pre = grad_hidden = 0.0
    for c, span in enumerate(spans):
        for copy in copies[c]:
            copy.wait()
        part_in = rows(c * chunk, chunk)
        gate_pre += plain(part_in, gate_w[span, :])
        up_pre += plain(part_in, up_w[span, :])
        grad_hidden += turned(rows(width + c * chunk, chunk), down_w[:, span])
    sigmoid_val = jax.nn.sigmoid(gate_pre)
    activated = gate_pre * sigmoid_val
    slope = sigmoid_val * (1.0 + gate_pre * (1.0 - sigmoid_val))
    hidden = (activated * up_pre).astype(jnp.bfloat16).astype(jnp.float32)
    gate_partial = jnp.sum(hidden * grad_hidden, axis=1, keepdims=True)
    scaled = flat_gate * grad_hidden
    grad_gate_pre = (scaled * up_pre * slope).astype(jnp.bfloat16)
    grad_up_pre = (scaled * activated).astype(jnp.bfloat16)
    da_ref[...] = grad_gate_pre
    du_ref[...] = grad_up_pre
    hw_ref[...] = (flat_gate * hidden).astype(jnp.bfloat16)
    term_ref[...] = jnp.where(named, gate_partial, 0.0).astype(jnp.bfloat16)


def rows_kernel(da_ref, du_ref, term_ref, gate_w, up_w, mine_ref, send_ref, *, width, chunk):
    half = mine_ref.shape[0]
    da, du = da_ref[...], du_ref[...]

    def turned(a, b):
        return lax.dot_general(a, b, CONTRACT_COLS, preferred_element_type=jnp.float32)

    for c in range(width // chunk):
        span = pl.ds(c * chunk, chunk)
        part = turned(da, gate_w[span, :]) + turned(du, up_w[span, :])
        part = part.astype(jnp.bfloat16)
        mine_ref[:, span] = part[:half]
        send_ref[:, span] = part[half:]
    last = pl.ds(width, LANES)
    mine_ref[:, last] = term_ref[:half, :]
    send_ref[:, last] = term_ref[half:, :]


def hidden_terms(held, other, weights, loads):
    count, columns = held.shape
    width, hid = weights[0].shape
    chunk = next(c for c in (1024, 512, 256, 128) if width % c == 0)
    me = lax.axis_index("node").astype(jnp.int32).reshape(1)
    unit = jax.ShapeDtypeStruct((2 * count, hid), jnp.bfloat16)
    shapes = (unit, unit, unit, jax.ShapeDtypeStruct((2 * count, LANES), jnp.bfloat16))
    if loads:
        shapes += tuple(pltpu.VMEM(w.shape, w.dtype) for w in weights)
    space = pl.ANY if loads else pltpu.VMEM
    place = in_hbm if loads else in_vmem
    *terms, = pl.pallas_call(
        functools.partial(hidden_kernel, width=width, chunk=chunk, loads=loads),
        out_shape=shapes,
        in_specs=[
            pl.BlockSpec(memory_space=pltpu.SMEM),
            *whole(2),
            *(pl.BlockSpec(memory_space=space),) * 3,
        ],
        out_specs=whole(len(shapes)),
        scratch_shapes=[pltpu.SemaphoreType.DMA((3, width // chunk))] if loads else [],
        compiler_params=pltpu.CompilerParams(vmem_limit_bytes=8 << 20),
        cost_estimate=NO_COST,
    )(me, held, other, *(place(w) for w in weights))
    return terms[:4], terms[4:] or weights


def row_terms(hidden, weights):
    da, du, _, term = hidden
    width = weights[0].shape[0]
    chunk = next(c for c in (1024, 512, 256, 128) if width % c == 0)
    back = jax.ShapeDtypeStruct((da.shape[0] // 2, width + LANES), jnp.bfloat16)
    return pl.pallas_call(
        functools.partial(rows_kernel, width=width, chunk=chunk),
        out_shape=(back, back),
        in_specs=list(whole(5)),
        out_specs=whole(2),
        compiler_params=pltpu.CompilerParams(vmem_limit_bytes=8 << 20),
        cost_estimate=NO_COST,
    )(da, du, term, *(in_vmem(w) for w in weights[:2]))


def dense(tokens, grad_out, expert_ids, gate_weights, w_gate, w_up, w_down):
    tok_count, width = tokens.shape
    node_count = lax.axis_size("node")
    local_count = lax.axis_size("local")
    clock = []

    def tick(*values):
        held = lax.optimization_barrier((*values, *clock))[: len(values)]
        return held[0] if len(values) == 1 else held

    def tock(value):
        clock[:] = [value]
        return value

    def permute(value, target):
        pairs = []
        for node in range(node_count):
            for place in range(local_count):
                to_node, to_place = target(node, place)
                pairs.append((node * local_count + place, to_node * local_count + to_place))
        return lax.ppermute(value, AXES, pairs)

    def cross(value, step):
        return permute(value, lambda n, p: (n ^ (2 if (n % 2 == 0) == (step == 0) else 4), p))

    def sibling(value):
        return permute(value, lambda n, p: (n ^ 1, p))

    def rotate(value, k):
        return permute(value, lambda n, p: (n, (p + k) % local_count))

    def along(value, bits):
        return permute(value, lambda n, p: (n, p ^ bits))

    def joined(*values):
        return jnp.concatenate(values, axis=1)

    own = pack(tokens, grad_out, expert_ids, gate_weights)[None, None]


    def terms(held, other, weights, loads):
        flat = [v.reshape(-1, v.shape[-1]) for v in (held, other)]
        return hidden_terms(*flat, weights, loads)

    def summed(mine, received):
        total = mine.astype(jnp.float32) + received.astype(jnp.float32)
        return total.reshape(-1, 4, tok_count, total.shape[-1]).astype(jnp.bfloat16)

    def folded(total, received):
        keep = received.shape[1]
        return (total[:, :keep].astype(jnp.float32) + received.astype(jnp.float32)).astype(jnp.bfloat16)

    def upper(total):
        return total[:, total.shape[1] // 2 :]


    weights = (w_gate[0], w_up[0], w_down[0])
    u_in = rotate(own, -1)
    v_in = rotate(own, 1)
    near_x = cross(own, 0)
    near_y = cross(own, 1)
    u = tock(tick(u_in))
    u_x = cross(u, 0)
    w_in = rotate(u, -1)
    near, near_x, near_y = tick(own, near_x, near_y)
    near = tock(joined(near, near_x, near_y))
    near_xy = cross(near_x, 1)
    v = tock(tick(v_in))
    v_x = cross(v, 0)
    u = tock(joined(*tick(u, u_x)))
    u_y = cross(u, 1)
    w = tock(tick(w_in))
    w_x = cross(w, 0)
    weights = load(*tick(*weights, own)[:3])
    tock(weights[0])
    v = tock(joined(*tick(v, v_x)))
    v_y = cross(v, 1)
    near = tock(joined(*tick(near, near_xy)))
    u = joined(*tick(u, u_y))
    first = tock(jnp.concatenate((near, u), axis=0))
    first_other = sibling(first)
    w = tock(joined(*tick(w, w_x)))
    w_y = cross(w, 1)
    first_hidden, weights = terms(*tick(first, first_other), weights, False)
    tock(first_hidden[0])
    first_mine, first_send = row_terms([tick(first_hidden[0]), *first_hidden[1:]], weights)
    tock(first_mine)
    first_back = sibling(first_send)
    v = tock(joined(*tick(v, v_y)))
    w = joined(*tick(w, w_y))
    second = tock(jnp.concatenate((v, w), axis=0))
    second_other = sibling(second)
    first_sum = tock(summed(*tick(first_mine, first_back)))
    first_r1 = cross(upper(first_sum), 1)
    second_hidden, _ = terms(*tick(second, second_other), weights, False)
    tock(second_hidden[0])
    second_mine, second_send = row_terms([tick(second_hidden[0]), *second_hidden[1:]], weights)
    tock(second_mine)
    second_back = [sibling(v) for v in jnp.split(second_send, 1)]
    first_sum = tock(folded(*tick(first_sum, first_r1)))
    first_sum = tock(tick(first_sum))
    first_r2 = cross(upper(first_sum), 0)
    second_mine, *second_back = tick(second_mine, *second_back)
    second_sum = tock(summed(second_mine, jnp.concatenate(second_back, axis=0)))
    cut = width // 2
    lo, hi = second_sum[..., :cut], second_sum[..., cut:]
    lo_r1 = cross(upper(lo), 1)
    hi_r1 = cross(upper(hi), 1)
    lo = tock(folded(*tick(lo, lo_r1)))
    lo_r2 = cross(upper(lo), 0)
    first_sum = tock(folded(*tick(first_sum, first_r2)))
    from_u = rotate(first_sum[1], 1)
    hi = tock(folded(*tick(hi, hi_r1)))
    hi_r2 = cross(upper(hi), 0)
    lo, lo_r2, hi, hi_r2 = tick(lo, lo_r2, hi, hi_r2)
    second_sum = tock(jnp.concatenate((folded(lo, lo_r2), folded(hi, hi_r2)), axis=-1))
    from_v = rotate(second_sum[0], -1)
    from_w = rotate(second_sum[1], 2)
    rows = [r.reshape(-1, r.shape[-1]) for r in (first, first_other, second, second_other)]
    rows[0] = tick(rows[0])
    sides = [[t[i] for t in (first_hidden, second_hidden)] for i in (0, 1, 2)]
    grad_gate_w, grad_up_w, grad_down = weight_terms(rows, *sides, width)
    tock(grad_down)
    from_u = tock(tick(from_u))
    ends = tick(first_sum[0], from_u, from_v, from_w)
    grad_in, grad_gate = finish([e[0] for e in ends], expert_ids)
    return (grad_in, grad_gate, grad_gate_w[None], grad_up_w[None], grad_down[None])


def slotted(tokens, grad_out, expert_ids, gate_weights, w_gate, w_up, w_down):
    tok_count = tokens.shape[0]
    width = tokens.shape[1]
    top_count = expert_ids.shape[1]
    node_count = lax.axis_size("node")
    local_count = lax.axis_size("local")
    capacity = max(2, 2 * tok_count * top_count // node_count)
    onehot = (
        expert_ids[:, :, None] == jnp.arange(node_count, dtype=jnp.int32)[None, None, :]
    ).astype(jnp.int32)
    per_token = jnp.sum(onehot, axis=1)
    earlier = jnp.cumsum(per_token, axis=0) - per_token
    slot_index = jnp.sum(earlier[:, None, :] * onehot, axis=2)
    flat_slot = expert_ids * capacity + slot_index
    placing = (
        flat_slot[:, :, None] == jnp.arange(node_count * capacity, dtype=jnp.int32)[None, None, :]
    ).astype(jnp.float32)
    placing_tok = jnp.sum(placing, axis=1).astype(jnp.bfloat16)
    send_in = (
        jnp.dot(placing_tok.T, tokens, preferred_element_type=jnp.float32)
        .astype(jnp.bfloat16)
        .reshape(node_count, capacity, width)
    )
    send_grad = (
        jnp.dot(placing_tok.T, grad_out, preferred_element_type=jnp.float32)
        .astype(jnp.bfloat16)
        .reshape(node_count, capacity, width)
    )
    send_gate = (
        jnp.einsum(
            "tks,tk->s", placing, gate_weights.astype(jnp.float32), precision=lax.Precision.HIGHEST
        )
        .astype(jnp.bfloat16)
        .reshape(node_count, capacity)
    )
    recv_in, recv_grad, recv_gate = (
        lax.all_to_all(send_in, "node", split_axis=0, concat_axis=0, tiled=True),
        lax.all_to_all(send_grad, "node", split_axis=0, concat_axis=0, tiled=True),
        lax.all_to_all(send_gate, "node", split_axis=0, concat_axis=0, tiled=True),
    )
    rows_in, rows_grad, rows_gate = (
        lax.all_gather(recv_in[None], "local", axis=0, tiled=True),
        lax.all_gather(recv_grad[None], "local", axis=0, tiled=True),
        lax.all_gather(recv_gate[None], "local", axis=0, tiled=True),
    )
    rows_total = local_count * node_count * capacity
    flat_in = rows_in.reshape(rows_total, width)
    flat_grad = rows_grad.reshape(rows_total, width)
    flat_gate = rows_gate.reshape(rows_total).astype(jnp.float32)
    gate_proj = w_gate[0]
    up_proj = w_up[0]
    down_proj = w_down[0]
    contract_rows = (((0,), (0,)), ((), ()))
    contract_cols = (((1,), (1,)), ((), ()))
    gate_pre = jnp.dot(flat_in, gate_proj, preferred_element_type=jnp.float32)
    up_pre = jnp.dot(flat_in, up_proj, preferred_element_type=jnp.float32)
    sigmoid_val = jax.nn.sigmoid(gate_pre)
    activated = gate_pre * sigmoid_val
    slope = sigmoid_val * (1.0 + gate_pre * (1.0 - sigmoid_val))
    hidden = (activated * up_pre).astype(jnp.bfloat16)
    grad_hidden = lax.dot_general(
        flat_grad, down_proj, contract_cols, preferred_element_type=jnp.float32
    )
    gate_partial = jnp.sum(hidden.astype(jnp.float32) * grad_hidden, axis=1)
    scaled = flat_gate[:, None] * grad_hidden
    grad_gate_pre = (scaled * up_pre * slope).astype(jnp.bfloat16)
    grad_up_pre = (scaled * activated).astype(jnp.bfloat16)
    weighted = (flat_gate[:, None] * hidden.astype(jnp.float32)).astype(jnp.bfloat16)
    grad_down = lax.dot_general(
        weighted, flat_grad, contract_rows, preferred_element_type=jnp.float32
    ).astype(jnp.bfloat16)
    grad_gate_w = lax.dot_general(
        flat_in, grad_gate_pre, contract_rows, preferred_element_type=jnp.float32
    ).astype(jnp.bfloat16)
    grad_up_w = lax.dot_general(
        flat_in, grad_up_pre, contract_rows, preferred_element_type=jnp.float32
    ).astype(jnp.bfloat16)
    input_partial = lax.dot_general(
        grad_gate_pre, gate_proj, contract_cols, preferred_element_type=jnp.float32
    )
    input_partial = input_partial + lax.dot_general(
        grad_up_pre, up_proj, contract_cols, preferred_element_type=jnp.float32
    )
    input_blocks = input_partial.reshape(local_count, node_count, capacity, width)
    gate_blocks = gate_partial.reshape(local_count, node_count, capacity)
    summed_in, summed_gate = (
        lax.psum_scatter(
            input_blocks.astype(jnp.bfloat16), "local", scatter_dimension=0, tiled=True
        ).astype(jnp.float32),
        lax.psum_scatter(
            gate_blocks.astype(jnp.bfloat16), "local", scatter_dimension=0, tiled=True
        ).astype(jnp.float32),
    )
    back_in, back_gate = (
        lax.all_to_all(
            summed_in[0].astype(jnp.bfloat16), "node", split_axis=0, concat_axis=0, tiled=True
        ),
        lax.all_to_all(
            summed_gate[0].astype(jnp.bfloat16), "node", split_axis=0, concat_axis=0, tiled=True
        ),
    )
    grad_in = jnp.dot(
        placing_tok,
        back_in.reshape(node_count * capacity, width),
        preferred_element_type=jnp.float32,
    ).astype(jnp.bfloat16)
    grad_gate = jnp.einsum(
        "tks,s->tk",
        placing,
        back_gate.reshape(node_count * capacity).astype(jnp.float32),
        precision=lax.Precision.HIGHEST,
    ).astype(jnp.bfloat16)
    return (grad_in, grad_gate, grad_gate_w[None], grad_up_w[None], grad_down[None])


def per_device(tokens, grad_out, expert_ids, gate_weights, w_gate, w_up, w_down):
    tok_count, top_count = expert_ids.shape
    node_count = lax.axis_size("node")
    capacity = max(2, 2 * tok_count * top_count // node_count)
    paired = node_count == 8 and lax.axis_size("local") == 4
    plan = dense if capacity >= tok_count and paired else slotted
    return plan(tokens, grad_out, expert_ids, gate_weights, w_gate, w_up, w_down)


def solution(mesh):
    placed = (
        P(("node", "local"), None),
        P(("node", "local"), None),
        P(("node", "local"), None),
        P(("node", "local"), None),
        P("node", None, "local"),
        P("node", None, "local"),
        P("node", "local", None),
    )
    return jax.shard_map(
        per_device,
        mesh=mesh,
        in_specs=placed,
        out_specs=(
            P(("node", "local"), None),
            P(("node", "local"), None),
            P("node", None, "local"),
            P("node", None, "local"),
            P("node", "local", None),
        ),
        check_vma=False,
    )
```
